32 devices in a mesh: gx: 2 (over y), gy: 2 (over core), vert: 8 (over z, x).
Axes of the slice: x: 2, y: 2, z: 4, core: 2. Of those that a mesh axis runs over, the one named last changes fastest.
Arguments:
- distribution: float32 [8000, 64, 256], P('vert', 'gx', 'gy'), may hold values from 0 to 13, as said below
- collision_rate: float32 [64, 256], P('gx', 'gy'), may hold values from 0.05 to 0.9
Outputs:
- advanced: float32 [8000, 64, 256], P('vert', 'gx', 'gy')
The draws below stay inside these ranges and needn't reach their ends.
Inputs may be any that keep to these rules, and one draw needn't show every extreme that they name: `distribution`: Nonnegative, of the shape of a local equilibrium with cell-to-cell variation.
All inputs are finite; a program needn't handle non-finite values.
Results may differ from the reference program's by a relative error of at most 0.0003.
Values sent between devices are 32-bit elements; how exact they have to be, the bound alone decides.
A program may use at most 384 MiB of HBM per device.

```python
import math
import jax
import jax.numpy as jnp
from jax import lax

VG = 20
NZ = 2
STEPS = 2
VEL = 8000
NX = 64
NY = 128


def draw_distribution(key, part):
    keys = jax.random.split(jax.random.fold_in(key, 7), 6)
    shape = (NX, NY * NZ)
    density = jnp.exp(jax.random.uniform(keys[0], shape, jnp.float32, jnp.log(0.5), jnp.log(2.0)))
    flow_x = jax.random.uniform(keys[1], shape, jnp.float32, -0.6, 0.6)
    flow_y = jax.random.uniform(keys[2], shape, jnp.float32, -0.6, 0.6)
    flow_z = jax.random.uniform(keys[3], shape, jnp.float32, -0.6, 0.6)
    temper = jax.random.uniform(keys[4], shape, jnp.float32, 0.6, 1.5)
    noise = jax.random.uniform(keys[5], (VEL, NX, NY * NZ), jnp.float32, -0.4, 0.4)
    labels = jnp.arange(VEL, dtype=jnp.int32)

    def speed(index):
        return (4.5 * (2.0 * (index.astype(jnp.float32) + 0.5) / VG - 1.0))[:, None, None]
    diff_x = speed(labels // (VG * VG)) - flow_x[None]
    diff_y = speed(labels // VG % VG) - flow_y[None]
    diff_z = speed(labels % VG) - flow_z[None]
    amplitude = density / (temper * jnp.sqrt(temper))
    shape_part = jnp.exp(-(diff_x * diff_x + diff_y * diff_y + diff_z * diff_z) / (2.0 * temper[None]))
    return amplitude[None] * shape_part * (1.0 + noise)


def steps_of(stream_key, extent, pieces, smallest, high):
    def one(axis_at, shards_of):
        heights = jax.random.uniform(jax.random.fold_in(jax.random.fold_in(stream_key, 6), axis_at), (shards_of,), jnp.float32, smallest / len(pieces), high / len(pieces))
        return jnp.repeat(jnp.exp(heights), extent[axis_at] // shards_of).reshape((-1,) + (1,) * (len(extent) - axis_at - 1))

    factor_of = one(*pieces[0])
    for cut in pieces[1:]:
        factor_of = factor_of * one(*cut)
    return factor_of


def setup_inputs(seed: int = 0) -> dict:
    key_list = jax.random.split(jax.random.key(seed), 3)
    return {
        "distribution": draw_distribution(jax.random.fold_in(key_list[2], 71), 0),
        "collision_rate": jnp.clip(jnp.exp(math.log(0.9) - 2.8903717 * jax.random.uniform(key_list[1], (NX, NY * NZ), jnp.float32) ** steps_of(key_list[1], (NX, NY * NZ), ((0, 2), (1, 2)), -0.2, 0.2)), 0.05, 0.9),
    }


speed_max = 4.5
time_step = 0.3 / 4.5

def grid_speed(index):
    return speed_max * (2.0 * (index.astype(jnp.float32) + 0.5) / VG - 1.0)

def velocity_tables(first, count):
    labels = first + jnp.arange(count, dtype=jnp.int32)
    speed_x = grid_speed(labels // (VG * VG))
    speed_y = grid_speed(labels // VG % VG)
    speed_z = grid_speed(labels % VG)
    weight = (2.0 * speed_max / VG) ** 3 / (2.0 * math.pi) ** 1.5
    table = jnp.stack([weight * jnp.ones_like(speed_x), weight * speed_x, weight * speed_y, weight * speed_z, weight * (speed_x * speed_x + speed_y * speed_y + speed_z * speed_z)])
    return (speed_x, speed_y, speed_z, table)

def running(center, xpad, ypad, speed_x, speed_y, speed_z):
    shaped = (-1, 1, 1, 1)
    speed_x = speed_x.reshape(shaped)
    speed_y = speed_y.reshape(shaped)
    speed_z = speed_z.reshape(shaped)
    back_x = (3.0 * center - 4.0 * xpad[:, 1:-3] + xpad[:, :-4]) * 0.5
    ahead_x = (-3.0 * center + 4.0 * xpad[:, 3:-1] - xpad[:, 4:]) * 0.5
    back_y = (3.0 * center - 4.0 * ypad[:, :, 1:-3] + ypad[:, :, :-4]) * 0.5
    ahead_y = (-3.0 * center + 4.0 * ypad[:, :, 3:-1] - ypad[:, :, 4:]) * 0.5
    back_z = (3.0 * center - 4.0 * jnp.roll(center, 1, 3) + jnp.roll(center, 2, 3)) * 0.5
    ahead_z = (-3.0 * center + 4.0 * jnp.roll(center, -1, 3) - jnp.roll(center, -2, 3)) * 0.5
    flux = jnp.maximum(speed_x, 0.0) * back_x + jnp.minimum(speed_x, 0.0) * ahead_x
    flux = flux + jnp.maximum(speed_y, 0.0) * back_y + jnp.minimum(speed_y, 0.0) * ahead_y
    flux = flux + jnp.maximum(speed_z, 0.0) * back_z + jnp.minimum(speed_z, 0.0) * ahead_z
    return center - time_step * flux

def parameters(moments):
    density = moments[0]
    flow_x = moments[1] / density
    flow_y = moments[2] / density
    flow_z = moments[3] / density
    temper = (moments[4] / density - (flow_x * flow_x + flow_y * flow_y + flow_z * flow_z)) / 3.0
    return jnp.stack([density / (temper * jnp.sqrt(temper)), flow_x, flow_y, flow_z, 0.5 / temper])

def relax(moved, speed_x, speed_y, speed_z, params, rate):
    diff_x = speed_x[:, None] - params[1][None]
    diff_y = speed_y[:, None] - params[2][None]
    diff_z = speed_z[:, None] - params[3][None]
    maxwell = params[0][None] * jnp.exp(-params[4][None] * (diff_x * diff_x + diff_y * diff_y + diff_z * diff_z))
    return moved + rate[None] * (maxwell - moved)

def reference(distribution, collision_rate):
    rate = collision_rate.reshape(-1)
    firsts = jnp.arange(VG, dtype=jnp.int32) * (VG * VG)
    state = distribution
    for step in range(STEPS):
        blocks = state.reshape(VG, VG * VG, NX, NY, NZ)

        def sweep(carry, item):
            block, first = item
            speed_x, speed_y, speed_z, table = velocity_tables(first, VG * VG)
            xpad = jnp.pad(block, ((0, 0), (2, 2), (0, 0), (0, 0)), mode='wrap')
            ypad = jnp.pad(block, ((0, 0), (0, 0), (2, 2), (0, 0)), mode='wrap')
            moved = running(block, xpad, ypad, speed_x, speed_y, speed_z).reshape(VG * VG, -1)
            carry = carry + jnp.dot(table, moved, precision=lax.Precision.HIGHEST)
            return (carry, moved)
        moments, moved_all = lax.scan(sweep, jnp.zeros((5, NX * NY * NZ), jnp.float32), (blocks, firsts))
        params = parameters(moments)

        def collide(item):
            moved, first = item
            speed_x, speed_y, speed_z, table = velocity_tables(first, VG * VG)
            return relax(moved, speed_x, speed_y, speed_z, params, rate)
        state = lax.map(collide, (moved_all, firsts)).reshape(VEL, NX, NY * NZ)
    return state
```

```python
import functools
import math

import jax
import jax.numpy as jnp
from jax import lax
from jax.experimental import pallas as pl
from jax.experimental.pallas import tpu as pltpu
from jax.sharding import PartitionSpec as P

VG = 20
NZ = 2
SPEED_MAX = 4.5
DT = 0.3 / 4.5
STEP = 2.0 * SPEED_MAX / VG
WEIGHT = STEP**3 / (2.0 * math.pi) ** 1.5
MESH = pl.DeviceIdType.MESH
HALF = VG // 2
SLAB = 4
PAD = 8


def speed_of(index):
    if isinstance(index, int):
        return STEP * (index + 0.5) - SPEED_MAX
    return STEP * (index.astype(jnp.float32) + 0.5) - SPEED_MAX


def group_place(first, group, size):
    start = first + group * size
    last = 0 if size == VG else lax.rem(start, VG)
    return start // (VG * VG), lax.rem(start // VG, VG), last


def amplitudes(ramp, flow_x, flow_y, inv, cx, cy):
    dx = cx - flow_x
    dy = cy - flow_y
    return ramp * jnp.exp(-inv * (dx * dx + dy * dy))


def stream(n_vert, size, chunk_groups, dist, rate, out, par_out, state, xs1, xh1, xs2, xh2, ys1, yh1, ys2, yh2,
           acc, mom, rs, pslab, ag, par, ez, hps, hpr, ezh, load_sem, out_sem,
           xs1_s, xs1_r, xs2_s, xs2_r, ys1_s, ys1_r, ys2_s, ys2_r, rs_s, rs_r, ag_s, ag_r, hp_s, hp_r):
    count, rows, cols = dist.shape
    groups = count // size
    chunks = groups // chunk_groups
    chunk_vel = chunk_groups * size
    owners = rows // SLAB
    gx, gy, me = lax.axis_index("gx"), lax.axis_index("gy"), lax.axis_index("vert")
    to_x = {"gx": 1 - gx}
    to_y = {"gy": 1 - gy}
    first = me * count
    x_up = me * 2 >= n_vert
    lane = lax.broadcasted_iota(jnp.int32, (rows, cols), 1)
    even = lane % NZ == 0
    slot = lane // (2 * NZ)

    def load(c):
        part = pl.ds(c * chunk_vel, chunk_vel)
        return pltpu.make_async_copy(dist.at[part], state.at[part, pl.ds(0, rows)], load_sem.at[c])

    def store(c):
        part = pl.ds(c * chunk_vel, chunk_vel)
        return pltpu.make_async_copy(state.at[part, pl.ds(0, rows)], out.at[part], out_sem.at[c])

    def send(src, dst, s_sem, r_sem, c, device):
        part = pl.ds(c * chunk_groups, chunk_groups)
        return pltpu.make_async_remote_copy(
            src_ref=src.at[part], dst_ref=dst.at[part], send_sem=s_sem.at[c], recv_sem=r_sem.at[c],
            device_id=device, device_id_type=MESH)

    def each(n, fn, low=0):
        lax.fori_loop(low, n, lambda c, z: (fn(c), z)[1], 0)

    each(chunks, lambda c: load(c).start())

    barrier = pltpu.get_barrier_semaphore()
    pl.semaphore_signal(barrier, inc=1, device_id=to_x, device_id_type=MESH)
    pl.semaphore_signal(barrier, inc=1, device_id=to_y, device_id_type=MESH)
    each(n_vert, lambda k: pl.semaphore_signal(
        barrier, inc=1, device_id={"vert": lax.rem(me + k, n_vert)}, device_id_type=MESH), 1)
    pl.semaphore_wait(barrier, n_vert + 1)

    def pack_chunk(c):
        load(c).wait()

        def pack(n, z):
            g = c * chunk_groups + n
            _, j, _ = group_place(first, g, size)
            turn = jnp.where(j >= HALF, 2 * NZ, 0)
            packed = jnp.zeros((rows, cols), jnp.float32)
            for t in range(size):
                v = g * size + t
                f = state[v, 0:rows, :]
                packed = jnp.where(slot == t, pltpu.roll(f, 2 * NZ * t + turn, 1), packed)
                xs1[g, 2 * t : 2 * t + 2, :] = jnp.where(x_up, f[rows - 2 : rows], f[0:2])
            ys1[g] = packed
            return z

        lax.fori_loop(0, chunk_groups, pack, 0)
        send(xs1, xh1, xs1_s, xs1_r, c, to_x).start()
        send(ys1, yh1, ys1_s, ys1_r, c, to_y).start()

    each(chunks, pack_chunk)

    def move_group(g, up, xh, yh, xs):
        i, j, l0 = group_place(first, g, size)
        cx, cy = speed_of(i), speed_of(j)
        ax, ay = DT * jnp.abs(cx), DT * jnp.abs(cy)
        y_up = j >= HALF
        turn = jnp.where(y_up, 2 * NZ, 0)
        near = jnp.where(y_up, NZ, cols - NZ)
        far = jnp.where(y_up, 2 * NZ, cols - 2 * NZ)
        edge = lax.rem(lane + turn, cols)
        edge_near = jnp.where(y_up, edge - NZ, edge)
        in_far = edge < 2 * NZ
        in_near = (edge_near >= 0) & (edge_near < NZ)
        base = 1.0 - 1.5 * ax - 1.5 * ay
        halo = yh[g]
        a = b = d = jnp.zeros((rows, cols), jnp.float32)
        tall = rows + PAD
        at = tall - 2 if up else rows
        for t in range(size):
            v = g * size + t
            state[v, at : at + 2, :] = xh[g, 2 * t : 2 * t + 2, :]
        for t in range(size):
            v = g * size + t
            az = 2.0 * DT * (abs(speed_of(t)) if size == VG else jnp.abs(speed_of(l0 + t)))
            whole = state[v]
            f = whole[0:rows]
            near_x = pltpu.roll(whole, 1 if up else tall - 1, 0)[0:rows]
            far_x = pltpu.roll(whole, 2 if up else tall - 2, 0)[0:rows]
            other = jnp.where(even, pltpu.roll(f, cols - 1, 1), pltpu.roll(f, 1, 1))
            edge_f = pltpu.roll(halo, lax.rem(2 * cols - 2 * NZ * t - turn, cols), 1)
            near_y = pltpu.roll(jnp.where(in_near, edge_f, f), near, 1)
            far_y = pltpu.roll(jnp.where(in_far, edge_f, f), far, 1)
            m = (base - az) * f + (2.0 * ax) * near_x - (0.5 * ax) * far_x
            m = m + ((2.0 * ay) * near_y - (0.5 * ay) * far_y + az * other)
            state[v, 0:rows, :] = m
            if xs is not None:
                xs[g, 2 * t : 2 * t + 2, :] = m[rows - 2 : rows] if up else m[0:2]
            a = a + m
            b = b + a
            d = d + b
        e = speed_of(l0) + STEP * size
        acc[0] += a
        acc[1] += cx * a
        acc[2] += cy * a
        acc[3] += e * a - STEP * b
        acc[4] += (cx * cx + cy * cy + e * e) * a - (2.0 * STEP * e + STEP * STEP) * b + (2.0 * STEP * STEP) * d

    def reduce_moments(step):
        for o in range(owners):
            for p in range(5):
                mom[o, p] = acc[p, SLAB * o : SLAB * (o + 1), :]

        def to_owner(o):
            return pltpu.make_async_remote_copy(
                src_ref=mom.at[o], dst_ref=rs.at[step, me], send_sem=rs_s.at[step, o], recv_sem=rs_r.at[step, me],
                device_id={"vert": o}, device_id_type=MESH)

        def from_device(s):
            return pltpu.make_async_remote_copy(
                src_ref=mom.at[0], dst_ref=rs.at[step, s], send_sem=rs_s.at[step, 0], recv_sem=rs_r.at[step, s],
                device_id={"vert": s}, device_id_type=MESH)

        def spread(s):
            return pltpu.make_async_remote_copy(
                src_ref=pslab.at[step], dst_ref=ag.at[step, me], send_sem=ag_s.at[step, s],
                recv_sem=ag_r.at[step, me], device_id={"vert": s}, device_id_type=MESH)

        def from_owner(o):
            return pltpu.make_async_remote_copy(
                src_ref=pslab.at[step], dst_ref=ag.at[step, o], send_sem=ag_s.at[step, 0],
                recv_sem=ag_r.at[step, o], device_id={"vert": o}, device_id_type=MESH)

        def others_owning(fn):
            def one(k):
                o = lax.rem(me + k, n_vert)
                if n_vert <= owners:
                    fn(o)
                else:
                    pl.when(o < owners)(lambda: fn(o))
            each(n_vert, one, 1)

        def others(fn):
            each(n_vert, lambda k: fn(lax.rem(me + k, n_vert)), 1)

        others_owning(lambda o: to_owner(o).start())

        def own():
            others(lambda s: from_device(s).wait_recv())

            def add(k, total):
                return total + rs[step, lax.rem(me + k, n_vert)]

            total = lax.fori_loop(1, n_vert, add, mom[me])
            mass = total[0]
            ux, uy, uz = total[1] / mass, total[2] / mass, total[3] / mass
            temper = (total[4] / mass - (ux * ux + uy * uy + uz * uz)) / 3.0
            pslab[step, 0] = WEIGHT * mass / (temper * jnp.sqrt(temper))
            pslab[step, 1] = ux
            pslab[step, 2] = uy
            pslab[step, 3] = uz
            pslab[step, 4] = 0.5 / temper
            others(lambda s: spread(s).start())
            ag[step, me] = pslab[step]

        if n_vert <= owners:
            own()
        else:
            pl.when(me < owners)(own)
        others_owning(lambda o: from_owner(o).wait_recv())
        for o in range(owners):
            for p in range(5):
                par[p, SLAB * o : SLAB * (o + 1), :] = ag[step, o, p]
        others_owning(lambda o: to_owner(o).wait_send())
        if n_vert <= owners:
            others(lambda s: spread(s).wait_send())
        else:
            pl.when(me < owners)(lambda: others(lambda s: spread(s).wait_send()))

    def move_first(c):
        send(ys1, yh1, ys1_s, ys1_r, c, to_y).wait_recv()
        send(xs1, xh1, xs1_s, xs1_r, c, to_x).wait_recv()
        for up in (True, False):
            @pl.when(x_up if up else jnp.logical_not(x_up))
            def _():
                each(chunk_groups, lambda n: move_group(c * chunk_groups + n, up, xh1, yh1, xs2))
        send(xs2, xh2, xs2_s, xs2_r, c, to_x).start()

    acc[...] = jnp.zeros_like(acc)
    each(chunks, move_first)
    reduce_moments(0)

    keep = 1.0 - rate[...]
    ramp = rate[...] * par[0]
    for p, value in enumerate((keep, ramp, par[1], par[2], par[3], par[4])):
        two = jnp.where(x_up, value[rows - 2 : rows], value[0:2])
        for q in range(PAD // 2):
            hps[p, 2 * q : 2 * q + 2, :] = two
    edges = pltpu.make_async_remote_copy(
        src_ref=hps, dst_ref=hpr, send_sem=hp_s, recv_sem=hp_r, device_id=to_x, device_id_type=MESH)
    edges.start()

    def fill_ez(l):
        dz = speed_of(l) - par[3]
        ez[l] = jnp.exp(-par[4] * dz * dz)

    each(VG, fill_ez)

    def collide_chunk(c):
        def collide(n, z):
            g = c * chunk_groups + n
            i, j, l0 = group_place(first, g, size)
            turn = jnp.where(j >= HALF, 2 * NZ, 0)
            keep = 1.0 - rate[...]
            amp = amplitudes(rate[...] * par[0], par[1], par[2], par[4], speed_of(i), speed_of(j))
            packed = jnp.zeros((rows, cols), jnp.float32)
            for t in range(size):
                v = g * size + t
                f = keep * state[v, 0:rows, :] + amp * ez[l0 + t]
                state[v, 0:rows, :] = f
                packed = jnp.where(slot == t, pltpu.roll(f, 2 * NZ * t + turn, 1), packed)
            ys2[g] = packed
            return z

        lax.fori_loop(0, chunk_groups, collide, 0)
        send(ys2, yh2, ys2_s, ys2_r, c, to_y).start()

    each(chunks, collide_chunk)

    edges.wait_recv()
    packed_rows = xh2.shape[1]
    for s in range(VG // size):
        for q in range(packed_rows // PAD):
            index = s * size + (lax.broadcasted_iota(jnp.int32, (PAD, cols), 0) + PAD * q) // 2
            dz = speed_of(index) - hpr[4]
            ezh[s, PAD * q : PAD * (q + 1), :] = jnp.exp(-hpr[5] * dz * dz)

    def collide_edge(g):
        i, j, l0 = group_place(first, g, size)
        amp = amplitudes(hpr[1], hpr[2], hpr[3], hpr[5], speed_of(i), speed_of(j))
        for q in range(packed_rows // PAD):
            part = slice(PAD * q, PAD * (q + 1))
            xh2[g, part, :] = hpr[0] * xh2[g, part, :] + amp * ezh[l0 // size, part, :]

    def move_second(c):
        send(ys2, yh2, ys2_s, ys2_r, c, to_y).wait_recv()
        send(xs2, xh2, xs2_s, xs2_r, c, to_x).wait_recv()
        each(chunk_groups, lambda n: collide_edge(c * chunk_groups + n))
        for up in (True, False):
            @pl.when(x_up if up else jnp.logical_not(x_up))
            def _():
                each(chunk_groups, lambda n: move_group(c * chunk_groups + n, up, xh2, yh2, None))
        store(c).start()

    acc[...] = jnp.zeros_like(acc)
    each(chunks, move_second)
    reduce_moments(1)
    par_out[...] = par[...]

    def finish(c):
        store(c).wait()
        send(xs1, xh1, xs1_s, xs1_r, c, to_x).wait_send()
        send(xs2, xh2, xs2_s, xs2_r, c, to_x).wait_send()
        send(ys1, yh1, ys1_s, ys1_r, c, to_y).wait_send()
        send(ys2, yh2, ys2_s, ys2_r, c, to_y).wait_send()

    each(chunks, finish)
    edges.wait_send()


def relax(size, chunk_groups, moved, rate, par, out, ez):
    step = pl.program_id(0)
    first = lax.axis_index("vert") * (pl.num_programs(0) * chunk_groups * size)

    @pl.when(step == 0)
    def _():
        def fill(l, z):
            dz = speed_of(l) - par[3]
            ez[l] = jnp.exp(-par[4] * dz * dz)
            return z
        lax.fori_loop(0, VG, fill, 0)

    def one(n, z):
        i, j, l0 = group_place(first, step * chunk_groups + n, size)
        keep = 1.0 - rate[...]
        amp = amplitudes(rate[...] * par[0], par[1], par[2], par[4], speed_of(i), speed_of(j))
        for t in range(size):
            out[n * size + t] = keep * moved[n * size + t] + amp * ez[l0 + t]
        return z

    lax.fori_loop(0, chunk_groups, one, 0)


def body(mesh, distribution, collision_rate):
    count, rows, cols = distribution.shape
    n_vert = mesh.shape["vert"]
    size = math.gcd(count, VG)
    groups = count // size
    chunk_groups = math.gcd(groups, 5)
    chunks = groups // chunk_groups
    packed_rows = -(-2 * size // PAD) * PAD
    owners = rows // SLAB
    f32 = jnp.float32
    x_edge = pltpu.VMEM((groups, packed_rows, cols), f32)
    y_edge = pltpu.VMEM((groups, rows, cols), f32)
    dma = pltpu.SemaphoreType.DMA
    vmem = pl.BlockSpec(memory_space=pltpu.VMEM)
    anywhere = pl.BlockSpec(memory_space=pl.ANY)
    moved, par = pl.pallas_call(
        functools.partial(stream, n_vert, size, chunk_groups),
        out_shape=(jax.ShapeDtypeStruct(distribution.shape, f32), jax.ShapeDtypeStruct((5, rows, cols), f32)),
        in_specs=[anywhere, vmem],
        out_specs=(anywhere, vmem),
        scratch_shapes=[
            pltpu.VMEM((count, rows + PAD, cols), f32),
            x_edge, x_edge, x_edge, x_edge,
            y_edge, y_edge, y_edge, y_edge,
            pltpu.VMEM((5, rows, cols), f32),
            pltpu.VMEM((owners, 5, SLAB, cols), f32),
            pltpu.VMEM((2, n_vert, 5, SLAB, cols), f32),
            pltpu.VMEM((2, 5, SLAB, cols), f32),
            pltpu.VMEM((2, owners, 5, SLAB, cols), f32),
            pltpu.VMEM((5, rows, cols), f32),
            pltpu.VMEM((VG, rows, cols), f32),
            pltpu.VMEM((6, PAD, cols), f32),
            pltpu.VMEM((6, PAD, cols), f32),
            pltpu.VMEM((VG // size, packed_rows, cols), f32),
        ]
        + [dma((chunks,))] * 10
        + [dma((2, owners)), dma((2, n_vert)), dma((2, n_vert)), dma((2, owners)), dma, dma],
        compiler_params=pltpu.CompilerParams(
            collective_id=0, has_side_effects=True, vmem_limit_bytes=56 * 1024 * 1024),
        name="stream",
    )(distribution, collision_rate)
    block = pl.BlockSpec((chunk_groups * size, rows, cols), lambda c: (c, 0, 0))
    return pl.pallas_call(
        functools.partial(relax, size, chunk_groups),
        out_shape=jax.ShapeDtypeStruct(distribution.shape, f32),
        grid=(chunks,),
        in_specs=[block, vmem, vmem],
        out_specs=block,
        scratch_shapes=[pltpu.VMEM((VG, rows, cols), f32)],
        compiler_params=pltpu.CompilerParams(vmem_limit_bytes=32 * 1024 * 1024),
        name="relax",
    )(moved, collision_rate, par)


def solution(mesh):
    placed = (P("vert", "gx", "gy"), P("gx", "gy"))
    return jax.shard_map(
        functools.partial(body, mesh), mesh=mesh, in_specs=placed, out_specs=P("vert", "gx", "gy"), check_vma=False)
```

```python
import functools
import math

import jax
import jax.numpy as jnp
from jax import lax
from jax.experimental import pallas as pl
from jax.experimental.pallas import tpu as pltpu
from jax.sharding import PartitionSpec as P

VG = 20
NZ = 2
SPEED_MAX = 4.5
DT = 0.3 / 4.5
STEP = 2.0 * SPEED_MAX / VG
WEIGHT = STEP**3 / (2.0 * math.pi) ** 1.5
MESH = pl.DeviceIdType.MESH
HALF = VG // 2
SLAB = 4
PAD = 8
SUB = 8
CHUNK = VG * VG // 2
BLOCK = 4


def speed_of(index):
    if isinstance(index, int):
        return STEP * (index + 0.5) - SPEED_MAX
    return STEP * (index.astype(jnp.float32) + 0.5) - SPEED_MAX


def group_place(first, group, size):
    start = first + group * size
    last = 0 if size == VG else lax.rem(start, VG)
    return start // (VG * VG), lax.rem(start // VG, VG), last


def amplitudes(ramp, flow_x, flow_y, inv, cx, cy):
    dx = cx - flow_x
    dy = cy - flow_y
    return ramp * jnp.exp(-inv * (dx * dx + dy * dy))


def stream(n_vert, size, chunk_groups, dist, rate, out, par_out, state, xs1, xh1, xs2, xh2, ys1, yh1, ys2, yh2,
           acc, mom, rs, pslab, ag, par, ez, hps, hpr, ezh, load_sem, out_sem,
           xs1_s, xs1_r, xs2_s, xs2_r, ys1_s, ys1_r, ys2_s, ys2_r, rs_s, rs_r, ag_s, ag_r, hp_s, hp_r):
    count, rows, cols = dist.shape
    groups = count // size
    chunks = groups // chunk_groups
    chunk_vel = chunk_groups * size
    owners = rows // SLAB
    gx, gy, me = lax.axis_index("gx"), lax.axis_index("gy"), lax.axis_index("vert")
    to_x = {"gx": 1 - gx}
    to_y = {"gy": 1 - gy}
    first = me * count
    x_up = me * 2 >= n_vert
    lane = lax.broadcasted_iota(jnp.int32, (rows, cols), 1)
    even = lane % NZ == 0
    slot = lane // (2 * NZ)

    def load(c):
        part = pl.ds(c * chunk_vel, chunk_vel)
        return pltpu.make_async_copy(dist.at[part], state.at[part, pl.ds(0, rows)], load_sem.at[c])

    def store(c):
        part = pl.ds(c * chunk_vel, chunk_vel)
        return pltpu.make_async_copy(state.at[part, pl.ds(0, rows)], out.at[part], out_sem.at[c])

    def send(src, dst, s_sem, r_sem, c, device):
        part = pl.ds(c * chunk_groups, chunk_groups)
        return pltpu.make_async_remote_copy(
            src_ref=src.at[part], dst_ref=dst.at[part], send_sem=s_sem.at[c], recv_sem=r_sem.at[c],
            device_id=device, device_id_type=MESH)

    def each(n, fn, low=0):
        lax.fori_loop(low, n, lambda c, z: (fn(c), z)[1], 0)

    each(chunks, lambda c: load(c).start())

    barrier = pltpu.get_barrier_semaphore()
    pl.semaphore_signal(barrier, inc=1, device_id=to_x, device_id_type=MESH)
    pl.semaphore_signal(barrier, inc=1, device_id=to_y, device_id_type=MESH)
    each(n_vert, lambda k: pl.semaphore_signal(
        barrier, inc=1, device_id={"vert": lax.rem(me + k, n_vert)}, device_id_type=MESH), 1)
    pl.semaphore_wait(barrier, n_vert + 1)

    def pack_chunk(c):
        load(c).wait()

        def pack(n, z):
            g = c * chunk_groups + n
            _, j, _ = group_place(first, g, size)
            turn = jnp.where(j >= HALF, 2 * NZ, 0)
            packed = jnp.zeros((rows, cols), jnp.float32)
            for t in range(size):
                v = g * size + t
                f = state[v, 0:rows, :]
                packed = jnp.where(slot == t, pltpu.roll(f, 2 * NZ * t + turn, 1), packed)
                xs1[g, 2 * t : 2 * t + 2, :] = jnp.where(x_up, f[rows - 2 : rows], f[0:2])
            ys1[g] = packed
            return z

        lax.fori_loop(0, chunk_groups, pack, 0)
        send(xs1, xh1, xs1_s, xs1_r, c, to_x).start()
        send(ys1, yh1, ys1_s, ys1_r, c, to_y).start()

    each(chunks, pack_chunk)

    def move_group(g, up, xh, yh, xs):
        i, j, l0 = group_place(first, g, size)
        cx, cy = speed_of(i), speed_of(j)
        ax, ay = DT * jnp.abs(cx), DT * jnp.abs(cy)
        y_up = j >= HALF
        turn = jnp.where(y_up, 2 * NZ, 0)
        near = jnp.where(y_up, NZ, cols - NZ)
        far = jnp.where(y_up, 2 * NZ, cols - 2 * NZ)
        edge = lax.rem(lane + turn, cols)
        edge_near = jnp.where(y_up, edge - NZ, edge)
        in_far = edge < 2 * NZ
        in_near = (edge_near >= 0) & (edge_near < NZ)
        base = 1.0 - 1.5 * ax - 1.5 * ay
        halo = yh[g]
        a = b = d = jnp.zeros((rows, cols), jnp.float32)
        tall = rows + PAD
        at = tall - 2 if up else rows
        for t in range(size):
            v = g * size + t
            state[v, at : at + 2, :] = xh[g, 2 * t : 2 * t + 2, :]
        for t in range(size):
            v = g * size + t
            az = 2.0 * DT * (abs(speed_of(t)) if size == VG else jnp.abs(speed_of(l0 + t)))
            whole = state[v]
            f = whole[0:rows]
            near_x = pltpu.roll(whole, 1 if up else tall - 1, 0)[0:rows]
            far_x = pltpu.roll(whole, 2 if up else tall - 2, 0)[0:rows]
            other = jnp.where(even, pltpu.roll(f, cols - 1, 1), pltpu.roll(f, 1, 1))
            edge_f = pltpu.roll(halo, lax.rem(2 * cols - 2 * NZ * t - turn, cols), 1)
            near_y = pltpu.roll(jnp.where(in_near, edge_f, f), near, 1)
            far_y = pltpu.roll(jnp.where(in_far, edge_f, f), far, 1)
            m = (base - az) * f + (2.0 * ax) * near_x - (0.5 * ax) * far_x
            m = m + ((2.0 * ay) * near_y - (0.5 * ay) * far_y + az * other)
            state[v, 0:rows, :] = m
            if xs is not None:
                xs[g, 2 * t : 2 * t + 2, :] = m[rows - 2 : rows] if up else m[0:2]
            a = a + m
            b = b + a
            d = d + b
        e = speed_of(l0) + STEP * size
        acc[0] += a
        acc[1] += cx * a
        acc[2] += cy * a
        acc[3] += e * a - STEP * b
        acc[4] += (cx * cx + cy * cy + e * e) * a - (2.0 * STEP * e + STEP * STEP) * b + (2.0 * STEP * STEP) * d

    def reduce_moments(step):
        for o in range(owners):
            for p in range(5):
                mom[o, p] = acc[p, SLAB * o : SLAB * (o + 1), :]

        def to_owner(o):
            return pltpu.make_async_remote_copy(
                src_ref=mom.at[o], dst_ref=rs.at[step, me], send_sem=rs_s.at[step, o], recv_sem=rs_r.at[step, me],
                device_id={"vert": o}, device_id_type=MESH)

        def from_device(s):
            return pltpu.make_async_remote_copy(
                src_ref=mom.at[0], dst_ref=rs.at[step, s], send_sem=rs_s.at[step, 0], recv_sem=rs_r.at[step, s],
                device_id={"vert": s}, device_id_type=MESH)

        def spread(s):
            return pltpu.make_async_remote_copy(
                src_ref=pslab.at[step], dst_ref=ag.at[step, me], send_sem=ag_s.at[step, s],
                recv_sem=ag_r.at[step, me], device_id={"vert": s}, device_id_type=MESH)

        def from_owner(o):
            return pltpu.make_async_remote_copy(
                src_ref=pslab.at[step], dst_ref=ag.at[step, o], send_sem=ag_s.at[step, 0],
                recv_sem=ag_r.at[step, o], device_id={"vert": o}, device_id_type=MESH)

        def others_owning(fn):
            def one(k):
                o = lax.rem(me + k, n_vert)
                if n_vert <= owners:
                    fn(o)
                else:
                    pl.when(o < owners)(lambda: fn(o))
            each(n_vert, one, 1)

        def others(fn):
            each(n_vert, lambda k: fn(lax.rem(me + k, n_vert)), 1)

        others_owning(lambda o: to_owner(o).start())

        def own():
            others(lambda s: from_device(s).wait_recv())

            def add(k, total):
                return total + rs[step, lax.rem(me + k, n_vert)]

            total = lax.fori_loop(1, n_vert, add, mom[me])
            mass = total[0]
            ux, uy, uz = total[1] / mass, total[2] / mass, total[3] / mass
            temper = (total[4] / mass - (ux * ux + uy * uy + uz * uz)) / 3.0
            pslab[step, 0] = WEIGHT * mass / (temper * jnp.sqrt(temper))
            pslab[step, 1] = ux
            pslab[step, 2] = uy
            pslab[step, 3] = uz
            pslab[step, 4] = 0.5 / temper
            others(lambda s: spread(s).start())
            ag[step, me] = pslab[step]

        if n_vert <= owners:
            own()
        else:
            pl.when(me < owners)(own)
        others_owning(lambda o: from_owner(o).wait_recv())
        for o in range(owners):
            for p in range(5):
                par[p, SLAB * o : SLAB * (o + 1), :] = ag[step, o, p]
        others_owning(lambda o: to_owner(o).wait_send())
        if n_vert <= owners:
            others(lambda s: spread(s).wait_send())
        else:
            pl.when(me < owners)(lambda: others(lambda s: spread(s).wait_send()))

    def move_first(c):
        send(ys1, yh1, ys1_s, ys1_r, c, to_y).wait_recv()
        send(xs1, xh1, xs1_s, xs1_r, c, to_x).wait_recv()
        for up in (True, False):
            @pl.when(x_up if up else jnp.logical_not(x_up))
            def _():
                each(chunk_groups, lambda n: move_group(c * chunk_groups + n, up, xh1, yh1, xs2))
        send(xs2, xh2, xs2_s, xs2_r, c, to_x).start()

    acc[...] = jnp.zeros_like(acc)
    each(chunks, move_first)
    reduce_moments(0)

    keep = 1.0 - rate[...]
    ramp = rate[...] * par[0]
    for p, value in enumerate((keep, ramp, par[1], par[2], par[3], par[4])):
        two = jnp.where(x_up, value[rows - 2 : rows], value[0:2])
        for q in range(PAD // 2):
            hps[p, 2 * q : 2 * q + 2, :] = two
    edges = pltpu.make_async_remote_copy(
        src_ref=hps, dst_ref=hpr, send_sem=hp_s, recv_sem=hp_r, device_id=to_x, device_id_type=MESH)
    edges.start()

    def fill_ez(l):
        dz = speed_of(l) - par[3]
        ez[l] = jnp.exp(-par[4] * dz * dz)

    each(VG, fill_ez)

    def collide_chunk(c):
        def collide(n, z):
            g = c * chunk_groups + n
            i, j, l0 = group_place(first, g, size)
            turn = jnp.where(j >= HALF, 2 * NZ, 0)
            keep = 1.0 - rate[...]
            amp = amplitudes(rate[...] * par[0], par[1], par[2], par[4], speed_of(i), speed_of(j))
            packed = jnp.zeros((rows, cols), jnp.float32)
            for t in range(size):
                v = g * size + t
                f = keep * state[v, 0:rows, :] + amp * ez[l0 + t]
                state[v, 0:rows, :] = f
                packed = jnp.where(slot == t, pltpu.roll(f, 2 * NZ * t + turn, 1), packed)
            ys2[g] = packed
            return z

        lax.fori_loop(0, chunk_groups, collide, 0)
        send(ys2, yh2, ys2_s, ys2_r, c, to_y).start()

    each(chunks, collide_chunk)

    edges.wait_recv()
    packed_rows = xh2.shape[1]
    for s in range(VG // size):
        for q in range(packed_rows // PAD):
            index = s * size + (lax.broadcasted_iota(jnp.int32, (PAD, cols), 0) + PAD * q) // 2
            dz = speed_of(index) - hpr[4]
            ezh[s, PAD * q : PAD * (q + 1), :] = jnp.exp(-hpr[5] * dz * dz)

    def collide_edge(g):
        i, j, l0 = group_place(first, g, size)
        amp = amplitudes(hpr[1], hpr[2], hpr[3], hpr[5], speed_of(i), speed_of(j))
        for q in range(packed_rows // PAD):
            part = slice(PAD * q, PAD * (q + 1))
            xh2[g, part, :] = hpr[0] * xh2[g, part, :] + amp * ezh[l0 // size, part, :]

    def move_second(c):
        send(ys2, yh2, ys2_s, ys2_r, c, to_y).wait_recv()
        send(xs2, xh2, xs2_s, xs2_r, c, to_x).wait_recv()
        each(chunk_groups, lambda n: collide_edge(c * chunk_groups + n))
        for up in (True, False):
            @pl.when(x_up if up else jnp.logical_not(x_up))
            def _():
                each(chunk_groups, lambda n: move_group(c * chunk_groups + n, up, xh2, yh2, None))
        store(c).start()

    acc[...] = jnp.zeros_like(acc)
    each(chunks, move_second)
    reduce_moments(1)
    par_out[...] = par[...]

    def finish(c):
        store(c).wait()
        send(xs1, xh1, xs1_s, xs1_r, c, to_x).wait_send()
        send(xs2, xh2, xs2_s, xs2_r, c, to_x).wait_send()
        send(ys1, yh1, ys1_s, ys1_r, c, to_y).wait_send()
        send(ys2, yh2, ys2_s, ys2_r, c, to_y).wait_send()

    each(chunks, finish)
    edges.wait_send()


def stream_rows(n_vert, dist, rate, out, par_out, T, U, ys1, yh1, ys2, yh2, tab, acc, mom, rs, pslab, ag, par, ez, ey,
                amp, hps, hpr, load_sem, out_sem, xs1_s, xs1_r, xs2_s, xs2_r, ys1_s, ys1_r, ys2_s, ys2_r,
                rs_s, rs_r, ag_s, ag_r, hp_s, hp_r):
    count, rows, cols = dist.shape
    chunks = count // CHUNK
    per_chunk = CHUNK // SUB
    gx, gy, me = lax.axis_index("gx"), lax.axis_index("gy"), lax.axis_index("vert")
    to_x = {"gx": 1 - gx}
    to_y = {"gy": 1 - gy}
    first = me * count
    x_up = me * 2 >= n_vert
    sign = jnp.where(x_up, 1, -1)
    start = jnp.where(x_up, 2, rows + 1)
    edge_from = jnp.where(x_up, rows, 2)
    edge_to = jnp.where(x_up, 0, rows + 2)
    lane = lax.broadcasted_iota(jnp.int32, (SUB, cols), 1)
    sub = lax.broadcasted_iota(jnp.int32, (SUB, cols), 0)
    even = lane % NZ == 0
    slot = lane // (2 * NZ)

    def row(k):
        return start + sign * k

    def each(n, fn, low=0):
        lax.fori_loop(low, n, lambda c, z: (fn(c), z)[1], 0)

    def span(c):
        return pl.ds(c * CHUNK, CHUNK)

    def load_start(c):
        each(rows, lambda x: pltpu.make_async_copy(
            dist.at[span(c), x, :], T.at[x + 2, span(c), :], load_sem.at[c]).start())

    def load_wait(c):
        inner = (pl.ds(2, rows), span(c))
        pltpu.make_async_copy(U.at[inner], T.at[inner], load_sem.at[c]).wait()

    def store_start(c):
        each(rows, lambda x: pltpu.make_async_copy(
            U.at[x + 2, span(c), :], out.at[span(c), x, :], out_sem.at[c]).start())

    def store_wait(c):
        inner = (pl.ds(2, rows), span(c))
        pltpu.make_async_copy(U.at[inner], T.at[inner], out_sem.at[c]).wait()

    def send_x(buf, s_sem, r_sem, c):
        return pltpu.make_async_remote_copy(
            src_ref=buf.at[pl.ds(edge_from, 2), span(c)], dst_ref=buf.at[pl.ds(edge_to, 2), span(c)],
            send_sem=s_sem.at[c], recv_sem=r_sem.at[c], device_id=to_x, device_id_type=MESH)

    def send_y(src, dst, s_sem, r_sem, c):
        part = pl.ds(c * per_chunk, per_chunk)
        return pltpu.make_async_remote_copy(
            src_ref=src.at[part], dst_ref=dst.at[part], send_sem=s_sem.at[c], recv_sem=r_sem.at[c],
            device_id=to_y, device_id_type=MESH)

    def chunk_place(c):
        begin = first + c * CHUNK
        return begin // (VG * VG), lax.rem(begin // CHUNK, 2)

    def by_half(half, fn):
        for up in (True, False):
            pl.when(half == (1 if up else 0))(functools.partial(fn, up))

    each(chunks, load_start)

    barrier = pltpu.get_barrier_semaphore()
    pl.semaphore_signal(barrier, inc=1, device_id=to_x, device_id_type=MESH)
    pl.semaphore_signal(barrier, inc=1, device_id=to_y, device_id_type=MESH)
    each(n_vert, lambda k: pl.semaphore_signal(
        barrier, inc=1, device_id={"vert": lax.rem(me + k, n_vert)}, device_id_type=MESH), 1)

    def fill_table(g):
        spot = (g * SUB + sub).astype(jnp.float32)
        j = jnp.floor((spot + 0.5) * (1.0 / VG))
        cy = STEP * (j + 0.5) - SPEED_MAX
        cz = STEP * (spot - VG * j + 0.5) - SPEED_MAX
        ay, az = DT * jnp.abs(cy), DT * jnp.abs(cz)
        tab[g, 0] = 1.0 - 1.5 * ay - 2.0 * az
        tab[g, 1] = 2.0 * ay
        tab[g, 2] = 2.0 * az
        tab[g, 3] = cy
        tab[g, 4] = cz
        tab[g, 5] = cy * cy + cz * cz

    each(2 * per_chunk, fill_table)
    pl.semaphore_wait(barrier, n_vert + 1)

    def pack_chunk(c):
        load_wait(c)
        send_x(T, xs1_s, xs1_r, c).start()
        _, half = chunk_place(c)

        def run(up):
            def pack(n):
                at = pl.ds(pl.multiple_of(c * CHUNK + n * SUB, SUB), SUB)
                packed = jnp.zeros((SUB, cols), jnp.float32)
                for k in range(rows):
                    turned = pltpu.roll(T[row(k), at, :], (2 * NZ * k + (2 * NZ if up else 0)) % cols, 1)
                    packed = jnp.where(slot == k, turned, packed)
                ys1[c * per_chunk + n] = packed

            each(per_chunk, pack)

        by_half(half, run)
        send_y(ys1, yh1, ys1_s, ys1_r, c).start()

    each(chunks, pack_chunk)

    def move_chunk(c, yh):
        i, half = chunk_place(c)
        cx = speed_of(i)
        ax = DT * jnp.abs(cx)

        def run(up):
            turn = 2 * NZ if up else 0
            near, far = (NZ, 2 * NZ) if up else (cols - NZ, cols - 2 * NZ)
            in_near = lane >= cols - NZ if up else lane < NZ
            in_far = lane >= cols - 2 * NZ if up else lane < 2 * NZ

            def block(kb):
                k0 = kb * BLOCK

                def five(sb, sums):
                    sums = list(sums)
                    for q in range(5):
                        n = sb * 5 + q
                        at = pl.ds(pl.multiple_of(c * CHUNK + n * SUB, SUB), SUB)
                        place = half * per_chunk + n
                        f = [T[row(k0 + kk), at, :] for kk in range(-2, BLOCK)]
                        c0 = tab[place, 0] - 1.5 * ax
                        by, bz = tab[place, 1], tab[place, 2]
                        cy, cz, cq = tab[place, 3], tab[place, 4], tab[place, 5]
                        halo = yh[c * per_chunk + n]
                        for kk in range(BLOCK):
                            far_x, near_x, mid = f[kk], f[kk + 1], f[kk + 2]
                            back = lax.rem(2 * cols - turn - 2 * NZ * (k0 + kk), cols)
                            edge = pltpu.roll(halo, back, 1)
                            near_y = pltpu.roll(jnp.where(in_near, edge, mid), near, 1)
                            far_y = pltpu.roll(jnp.where(in_far, edge, mid), far, 1)
                            other = jnp.where(even, pltpu.roll(mid, cols - 1, 1), pltpu.roll(mid, 1, 1))
                            m = (c0 * mid + (2.0 * ax) * (near_x - 0.25 * far_x)) + (
                                by * (near_y - 0.25 * far_y) + bz * other)
                            U[row(k0 + kk), at, :] = m
                            sums[4 * kk] = sums[4 * kk] + m
                            sums[4 * kk + 1] = sums[4 * kk + 1] + cy * m
                            sums[4 * kk + 2] = sums[4 * kk + 2] + cz * m
                            sums[4 * kk + 3] = sums[4 * kk + 3] + cq * m
                    return tuple(sums)

                zero = jnp.zeros((SUB, cols), jnp.float32)
                sums = lax.fori_loop(0, per_chunk // 5, five, (zero,) * (4 * BLOCK))
                for kk in range(BLOCK):
                    x = row(k0 + kk) - 2
                    a, my, mz, mq = sums[4 * kk : 4 * kk + 4]
                    acc[0, x] += a
                    acc[1, x] += cx * a
                    acc[2, x] += my
                    acc[3, x] += mz
                    acc[4, x] += (cx * cx) * a + mq

            each(rows // BLOCK, block)

        by_half(half, run)

    def reduce_moments(step):
        for o in range(n_vert):
            for p in range(5):
                mom[o, p] = jnp.sum(acc[p, SLAB * o : SLAB * (o + 1)], axis=1)

        def to_owner(o):
            return pltpu.make_async_remote_copy(
                src_ref=mom.at[o], dst_ref=rs.at[step, me], send_sem=rs_s.at[step, o], recv_sem=rs_r.at[step, me],
                device_id={"vert": o}, device_id_type=MESH)

        def from_device(s):
            return pltpu.make_async_remote_copy(
                src_ref=mom.at[s], dst_ref=rs.at[step, s], send_sem=rs_s.at[step, s], recv_sem=rs_r.at[step, s],
                device_id={"vert": s}, device_id_type=MESH)

        def spread(s):
            return pltpu.make_async_remote_copy(
                src_ref=pslab.at[step], dst_ref=ag.at[step, me], send_sem=ag_s.at[step, s],
                recv_sem=ag_r.at[step, me], device_id={"vert": s}, device_id_type=MESH)

        def from_owner(o):
            return pltpu.make_async_remote_copy(
                src_ref=pslab.at[step], dst_ref=ag.at[step, o], send_sem=ag_s.at[step, o],
                recv_sem=ag_r.at[step, o], device_id={"vert": o}, device_id_type=MESH)

        def others(fn):
            each(n_vert, lambda k: fn(lax.rem(me + k, n_vert)), 1)

        others(lambda o: to_owner(o).start())
        others(lambda s: from_device(s).wait_recv())
        total = lax.fori_loop(1, n_vert, lambda k, t: t + rs[step, lax.rem(me + k, n_vert)], mom[me])
        mass = total[0]
        ux, uy, uz = total[1] / mass, total[2] / mass, total[3] / mass
        temper = (total[4] / mass - (ux * ux + uy * uy + uz * uz)) / 3.0
        pslab[step, 0] = WEIGHT * mass / (temper * jnp.sqrt(temper))
        pslab[step, 1] = ux
        pslab[step, 2] = uy
        pslab[step, 3] = uz
        pslab[step, 4] = 0.5 / temper
        others(lambda s: spread(s).start())
        ag[step, me] = pslab[step]
        others(lambda o: from_owner(o).wait_recv())
        others(lambda o: to_owner(o).wait_send())
        others(lambda s: spread(s).wait_send())

    def move_first(c):
        send_y(ys1, yh1, ys1_s, ys1_r, c).wait_recv()
        send_x(T, xs1_s, xs1_r, c).wait_recv()
        move_chunk(c, yh1)
        send_x(U, xs2_s, xs2_r, c).start()

    acc[...] = jnp.zeros_like(acc)
    each(chunks, move_first)
    reduce_moments(0)

    par[...] = jnp.ones_like(par)
    par[0, 2 : rows + 2, :] = 1.0 - rate[...]
    for o in range(n_vert):
        at = slice(SLAB * o + 2, SLAB * (o + 1) + 2)
        par[1, at, :] = rate[SLAB * o : SLAB * (o + 1), :] * ag[0, o, 0]
        for p in range(1, 5):
            par[p + 1, at, :] = ag[0, o, p]
    for p in range(6):
        hps[p] = jnp.where(x_up, par[p, rows : rows + 2, :], par[p, 2:4, :])
    edges = pltpu.make_async_remote_copy(
        src_ref=hps, dst_ref=hpr, send_sem=hp_s, recv_sem=hp_r, device_id=to_x, device_id_type=MESH)
    edges.start()

    def fill_ey():
        def one(j):
            dy = speed_of(j) - par[3]
            ey[j] = jnp.exp(-par[5] * dy * dy)
        each(VG, one)

    def fill_ez(r):
        for q in range(5):
            dz = tab[q, 4] - par[4, pl.ds(r, 1), :]
            ez[q, r] = jnp.exp(-par[5, pl.ds(r, 1), :] * dz * dz)

    def fill_amp(c):
        i, half = chunk_place(c)
        dx = speed_of(i) - par[2]
        front = par[1] * jnp.exp(-par[5] * dx * dx)
        for j in range(VG // 2):
            amp[j] = front * ey[half * (VG // 2) + j]

    def collided(c, sb, r):
        low = jnp.broadcast_to(amp[2 * sb, pl.ds(r, 1), :], (SUB, cols))
        high = jnp.broadcast_to(amp[2 * sb + 1, pl.ds(r, 1), :], (SUB, cols))
        keep = jnp.broadcast_to(par[0, pl.ds(r, 1), :], (SUB, cols))
        mixed = jnp.where(sub < SUB // 2, low, high)
        found = []
        for q, front in enumerate((low, low, mixed, high, high)):
            at = pl.ds(pl.multiple_of(c * CHUNK + (sb * 5 + q) * SUB, SUB), SUB)
            f = keep * U[r, at, :] + front * ez[q, r]
            T[r, at, :] = f
            found.append(f)
        return found

    fill_ey()
    each(rows, lambda x: fill_ez(x + 2))

    def collide_chunk(c):
        send_x(T, xs1_s, xs1_r, c).wait_send()
        _, half = chunk_place(c)
        fill_amp(c)

        def run(up):
            def five(sb):
                def some(kb, packed):
                    packed = list(packed)
                    for kk in range(BLOCK):
                        k = kb * BLOCK + kk
                        turn = lax.rem(2 * NZ * k + (2 * NZ if up else 0), cols)
                        here = slot == k
                        for q, f in enumerate(collided(c, sb, row(k))):
                            packed[q] = jnp.where(here, pltpu.roll(f, turn, 1), packed[q])
                    return tuple(packed)

                zero = jnp.zeros((SUB, cols), jnp.float32)
                packed = lax.fori_loop(0, rows // BLOCK, some, (zero,) * 5)
                for q in range(5):
                    ys2[c * per_chunk + sb * 5 + q] = packed[q]

            each(per_chunk // 5, five)

        by_half(half, run)
        send_y(ys2, yh2, ys2_s, ys2_r, c).start()

    each(chunks, collide_chunk)

    edges.wait_recv()
    for p in range(6):
        par[p, 0:2, :] = hpr[p]
        par[p, rows + 2 : rows + 4, :] = hpr[p]
    fill_ey()
    each(2, lambda x: fill_ez(edge_to + x))

    def move_second(c):
        send_y(ys2, yh2, ys2_s, ys2_r, c).wait_recv()
        send_x(U, xs2_s, xs2_r, c).wait_recv()
        send_x(U, xs2_s, xs2_r, c).wait_send()
        fill_amp(c)

        def edge(sb):
            collided(c, sb, edge_to)
            collided(c, sb, edge_to + 1)

        each(per_chunk // 5, edge)
        move_chunk(c, yh2)
        store_start(c)

    acc[...] = jnp.zeros_like(acc)
    each(chunks, move_second)
    reduce_moments(1)
    for o in range(n_vert):
        for p in range(5):
            par_out[p, SLAB * o : SLAB * (o + 1), :] = ag[1, o, p]

    def finish(c):
        store_wait(c)
        send_y(ys1, yh1, ys1_s, ys1_r, c).wait_send()
        send_y(ys2, yh2, ys2_s, ys2_r, c).wait_send()

    each(chunks, finish)
    edges.wait_send()


def run_rows(n_vert, distribution, collision_rate):
    count, rows, cols = distribution.shape
    chunks, groups = count // CHUNK, count // SUB
    f32 = jnp.float32
    state = pltpu.VMEM((rows + 4, count, cols), f32)
    y_edge = pltpu.VMEM((groups, SUB, cols), f32)
    dma = pltpu.SemaphoreType.DMA
    vmem = pl.BlockSpec(memory_space=pltpu.VMEM)
    anywhere = pl.BlockSpec(memory_space=pl.ANY)
    return pl.pallas_call(
        functools.partial(stream_rows, n_vert),
        out_shape=(jax.ShapeDtypeStruct(distribution.shape, f32), jax.ShapeDtypeStruct((5, rows, cols), f32)),
        in_specs=[anywhere, vmem],
        out_specs=(anywhere, vmem),
        scratch_shapes=[
            state, state, y_edge, y_edge, y_edge, y_edge,
            pltpu.VMEM((2 * CHUNK // SUB, 6, SUB, cols), f32),
            pltpu.VMEM((5, rows, SUB, cols), f32),
            pltpu.VMEM((n_vert, 5, SLAB, cols), f32),
            pltpu.VMEM((2, n_vert, 5, SLAB, cols), f32),
            pltpu.VMEM((2, 5, SLAB, cols), f32),
            pltpu.VMEM((2, n_vert, 5, SLAB, cols), f32),
            pltpu.VMEM((6, rows + 4, cols), f32),
            pltpu.VMEM((5, rows + 4, SUB, cols), f32),
            pltpu.VMEM((VG, rows + 4, cols), f32),
            pltpu.VMEM((VG // 2, rows + 4, cols), f32),
            pltpu.VMEM((6, 2, cols), f32),
            pltpu.VMEM((6, 2, cols), f32),
        ]
        + [dma((chunks,))] * 10
        + [dma((2, n_vert))] * 4 + [dma, dma],
        compiler_params=pltpu.CompilerParams(
            collective_id=1, has_side_effects=True, vmem_limit_bytes=56 * 1024 * 1024),
        name="stream_rows",
    )(distribution, collision_rate)


def relax(size, chunk_groups, moved, rate, par, out, ez):
    step = pl.program_id(0)
    first = lax.axis_index("vert") * (pl.num_programs(0) * chunk_groups * size)

    @pl.when(step == 0)
    def _():
        def fill(l, z):
            dz = speed_of(l) - par[3]
            ez[l] = jnp.exp(-par[4] * dz * dz)
            return z
        lax.fori_loop(0, VG, fill, 0)

    def one(n, z):
        i, j, l0 = group_place(first, step * chunk_groups + n, size)
        keep = 1.0 - rate[...]
        amp = amplitudes(rate[...] * par[0], par[1], par[2], par[4], speed_of(i), speed_of(j))
        for t in range(size):
            out[n * size + t] = keep * moved[n * size + t] + amp * ez[l0 + t]
        return z

    lax.fori_loop(0, chunk_groups, one, 0)


def body(mesh, distribution, collision_rate):
    count, rows, cols = distribution.shape
    n_vert = mesh.shape["vert"]
    size = math.gcd(count, VG)
    groups = count // size
    chunk_groups = math.gcd(groups, 5)
    chunks = groups // chunk_groups
    packed_rows = -(-2 * size // PAD) * PAD
    owners = rows // SLAB
    f32 = jnp.float32
    x_edge = pltpu.VMEM((groups, packed_rows, cols), f32)
    y_edge = pltpu.VMEM((groups, rows, cols), f32)
    dma = pltpu.SemaphoreType.DMA
    vmem = pl.BlockSpec(memory_space=pltpu.VMEM)
    anywhere = pl.BlockSpec(memory_space=pl.ANY)
    if count % CHUNK == 0 and rows == SLAB * n_vert:
        moved, par = run_rows(n_vert, distribution, collision_rate)
    else:
        moved, par = pl.pallas_call(
            functools.partial(stream, n_vert, size, chunk_groups),
            out_shape=(jax.ShapeDtypeStruct(distribution.shape, f32), jax.ShapeDtypeStruct((5, rows, cols), f32)),
            in_specs=[anywhere, vmem],
            out_specs=(anywhere, vmem),
            scratch_shapes=[
                pltpu.VMEM((count, rows + PAD, cols), f32),
                x_edge, x_edge, x_edge, x_edge,
                y_edge, y_edge, y_edge, y_edge,
                pltpu.VMEM((5, rows, cols), f32),
                pltpu.VMEM((owners, 5, SLAB, cols), f32),
                pltpu.VMEM((2, n_vert, 5, SLAB, cols), f32),
                pltpu.VMEM((2, 5, SLAB, cols), f32),
                pltpu.VMEM((2, owners, 5, SLAB, cols), f32),
                pltpu.VMEM((5, rows, cols), f32),
                pltpu.VMEM((VG, rows, cols), f32),
                pltpu.VMEM((6, PAD, cols), f32),
                pltpu.VMEM((6, PAD, cols), f32),
                pltpu.VMEM((VG // size, packed_rows, cols), f32),
            ]
            + [dma((chunks,))] * 10
            + [dma((2, owners)), dma((2, n_vert)), dma((2, n_vert)), dma((2, owners)), dma, dma],
            compiler_params=pltpu.CompilerParams(
                collective_id=0, has_side_effects=True, vmem_limit_bytes=56 * 1024 * 1024),
            name="stream",
        )(distribution, collision_rate)
    block = pl.BlockSpec((chunk_groups * size, rows, cols), lambda c: (c, 0, 0))
    return pl.pallas_call(
        functools.partial(relax, size, chunk_groups),
        out_shape=jax.ShapeDtypeStruct(distribution.shape, f32),
        grid=(chunks,),
        in_specs=[block, vmem, vmem],
        out_specs=block,
        scratch_shapes=[pltpu.VMEM((VG, rows, cols), f32)],
        compiler_params=pltpu.CompilerParams(vmem_limit_bytes=60 * 1024 * 1024),
        name="relax",
    )(moved, collision_rate, par)


def solution(mesh):
    placed = (P("vert", "gx", "gy"), P("gx", "gy"))
    return jax.shard_map(
        functools.partial(body, mesh), mesh=mesh, in_specs=placed, out_specs=P("vert", "gx", "gy"), check_vma=False)
```

```python
import functools
import math

import jax
import jax.numpy as jnp
from jax import lax
from jax.experimental import pallas as pl
from jax.experimental.pallas import tpu as pltpu
from jax.sharding import PartitionSpec as P

VG = 20
NZ = 2
SPEED_MAX = 4.5
DT = 0.3 / 4.5
STEP = 2.0 * SPEED_MAX / VG
WEIGHT = STEP**3 / (2.0 * math.pi) ** 1.5
MESH = pl.DeviceIdType.MESH
HALF = VG // 2
SLAB = 4
PAD = 8
SUB = 8
CHUNK = VG * VG // 2
BLOCK = 4


def speed_of(index):
    if isinstance(index, int):
        return STEP * (index + 0.5) - SPEED_MAX
    return STEP * (index.astype(jnp.float32) + 0.5) - SPEED_MAX


def group_place(first, group, size):
    start = first + group * size
    last = 0 if size == VG else lax.rem(start, VG)
    return start // (VG * VG), lax.rem(start // VG, VG), last


def amplitudes(ramp, flow_x, flow_y, inv, cx, cy):
    dx = cx - flow_x
    dy = cy - flow_y
    return ramp * jnp.exp(-inv * (dx * dx + dy * dy))


def stream(n_vert, size, chunk_groups, dist, rate, out, par_out, state, xs1, xh1, xs2, xh2, ys1, yh1, ys2, yh2,
           acc, mom, rs, pslab, ag, par, ez, hps, hpr, ezh, load_sem, out_sem,
           xs1_s, xs1_r, xs2_s, xs2_r, ys1_s, ys1_r, ys2_s, ys2_r, rs_s, rs_r, ag_s, ag_r, hp_s, hp_r):
    count, rows, cols = dist.shape
    groups = count // size
    chunks = groups // chunk_groups
    chunk_vel = chunk_groups * size
    owners = rows // SLAB
    gx, gy, me = lax.axis_index("gx"), lax.axis_index("gy"), lax.axis_index("vert")
    to_x = {"gx": 1 - gx}
    to_y = {"gy": 1 - gy}
    first = me * count
    x_up = me * 2 >= n_vert
    lane = lax.broadcasted_iota(jnp.int32, (rows, cols), 1)
    even = lane % NZ == 0
    slot = lane // (2 * NZ)

    def load(c):
        part = pl.ds(c * chunk_vel, chunk_vel)
        return pltpu.make_async_copy(dist.at[part], state.at[part, pl.ds(0, rows)], load_sem.at[c])

    def store(c):
        part = pl.ds(c * chunk_vel, chunk_vel)
        return pltpu.make_async_copy(state.at[part, pl.ds(0, rows)], out.at[part], out_sem.at[c])

    def send(src, dst, s_sem, r_sem, c, device):
        part = pl.ds(c * chunk_groups, chunk_groups)
        return pltpu.make_async_remote_copy(
            src_ref=src.at[part], dst_ref=dst.at[part], send_sem=s_sem.at[c], recv_sem=r_sem.at[c],
            device_id=device, device_id_type=MESH)

    def each(n, fn, low=0):
        lax.fori_loop(low, n, lambda c, z: (fn(c), z)[1], 0)

    each(chunks, lambda c: load(c).start())

    barrier = pltpu.get_barrier_semaphore()
    pl.semaphore_signal(barrier, inc=1, device_id=to_x, device_id_type=MESH)
    pl.semaphore_signal(barrier, inc=1, device_id=to_y, device_id_type=MESH)
    each(n_vert, lambda k: pl.semaphore_signal(
        barrier, inc=1, device_id={"vert": lax.rem(me + k, n_vert)}, device_id_type=MESH), 1)
    pl.semaphore_wait(barrier, n_vert + 1)

    def pack_chunk(c):
        load(c).wait()

        def pack(n, z):
            g = c * chunk_groups + n
            _, j, _ = group_place(first, g, size)
            turn = jnp.where(j >= HALF, 2 * NZ, 0)
            packed = jnp.zeros((rows, cols), jnp.float32)
            for t in range(size):
                v = g * size + t
                f = state[v, 0:rows, :]
                packed = jnp.where(slot == t, pltpu.roll(f, 2 * NZ * t + turn, 1), packed)
                xs1[g, 2 * t : 2 * t + 2, :] = jnp.where(x_up, f[rows - 2 : rows], f[0:2])
            ys1[g] = packed
            return z

        lax.fori_loop(0, chunk_groups, pack, 0)
        send(xs1, xh1, xs1_s, xs1_r, c, to_x).start()
        send(ys1, yh1, ys1_s, ys1_r, c, to_y).start()

    each(chunks, pack_chunk)

    def move_group(g, up, xh, yh, xs):
        i, j, l0 = group_place(first, g, size)
        cx, cy = speed_of(i), speed_of(j)
        ax, ay = DT * jnp.abs(cx), DT * jnp.abs(cy)
        y_up = j >= HALF
        turn = jnp.where(y_up, 2 * NZ, 0)
        near = jnp.where(y_up, NZ, cols - NZ)
        far = jnp.where(y_up, 2 * NZ, cols - 2 * NZ)
        edge = lax.rem(lane + turn, cols)
        edge_near = jnp.where(y_up, edge - NZ, edge)
        in_far = edge < 2 * NZ
        in_near = (edge_near >= 0) & (edge_near < NZ)
        base = 1.0 - 1.5 * ax - 1.5 * ay
        halo = yh[g]
        a = b = d = jnp.zeros((rows, cols), jnp.float32)
        tall = rows + PAD
        at = tall - 2 if up else rows
        for t in range(size):
            v = g * size + t
            state[v, at : at + 2, :] = xh[g, 2 * t : 2 * t + 2, :]
        for t in range(size):
            v = g * size + t
            az = 2.0 * DT * (abs(speed_of(t)) if size == VG else jnp.abs(speed_of(l0 + t)))
            whole = state[v]
            f = whole[0:rows]
            near_x = pltpu.roll(whole, 1 if up else tall - 1, 0)[0:rows]
            far_x = pltpu.roll(whole, 2 if up else tall - 2, 0)[0:rows]
            other = jnp.where(even, pltpu.roll(f, cols - 1, 1), pltpu.roll(f, 1, 1))
            edge_f = pltpu.roll(halo, lax.rem(2 * cols - 2 * NZ * t - turn, cols), 1)
            near_y = pltpu.roll(jnp.where(in_near, edge_f, f), near, 1)
            far_y = pltpu.roll(jnp.where(in_far, edge_f, f), far, 1)
            m = (base - az) * f + (2.0 * ax) * near_x - (0.5 * ax) * far_x
            m = m + ((2.0 * ay) * near_y - (0.5 * ay) * far_y + az * other)
            state[v, 0:rows, :] = m
            if xs is not None:
                xs[g, 2 * t : 2 * t + 2, :] = m[rows - 2 : rows] if up else m[0:2]
            a = a + m
            b = b + a
            d = d + b
        e = speed_of(l0) + STEP * size
        acc[0] += a
        acc[1] += cx * a
        acc[2] += cy * a
        acc[3] += e * a - STEP * b
        acc[4] += (cx * cx + cy * cy + e * e) * a - (2.0 * STEP * e + STEP * STEP) * b + (2.0 * STEP * STEP) * d

    def reduce_moments(step):
        for o in range(owners):
            for p in range(5):
                mom[o, p] = acc[p, SLAB * o : SLAB * (o + 1), :]

        def to_owner(o):
            return pltpu.make_async_remote_copy(
                src_ref=mom.at[o], dst_ref=rs.at[step, me], send_sem=rs_s.at[step, o], recv_sem=rs_r.at[step, me],
                device_id={"vert": o}, device_id_type=MESH)

        def from_device(s):
            return pltpu.make_async_remote_copy(
                src_ref=mom.at[0], dst_ref=rs.at[step, s], send_sem=rs_s.at[step, 0], recv_sem=rs_r.at[step, s],
                device_id={"vert": s}, device_id_type=MESH)

        def spread(s):
            return pltpu.make_async_remote_copy(
                src_ref=pslab.at[step], dst_ref=ag.at[step, me], send_sem=ag_s.at[step, s],
                recv_sem=ag_r.at[step, me], device_id={"vert": s}, device_id_type=MESH)

        def from_owner(o):
            return pltpu.make_async_remote_copy(
                src_ref=pslab.at[step], dst_ref=ag.at[step, o], send_sem=ag_s.at[step, 0],
                recv_sem=ag_r.at[step, o], device_id={"vert": o}, device_id_type=MESH)

        def others_owning(fn):
            def one(k):
                o = lax.rem(me + k, n_vert)
                if n_vert <= owners:
                    fn(o)
                else:
                    pl.when(o < owners)(lambda: fn(o))
            each(n_vert, one, 1)

        def others(fn):
            each(n_vert, lambda k: fn(lax.rem(me + k, n_vert)), 1)

        others_owning(lambda o: to_owner(o).start())

        def own():
            others(lambda s: from_device(s).wait_recv())

            def add(k, total):
                return total + rs[step, lax.rem(me + k, n_vert)]

            total = lax.fori_loop(1, n_vert, add, mom[me])
            mass = total[0]
            ux, uy, uz = total[1] / mass, total[2] / mass, total[3] / mass
            temper = (total[4] / mass - (ux * ux + uy * uy + uz * uz)) / 3.0
            pslab[step, 0] = WEIGHT * mass / (temper * jnp.sqrt(temper))
            pslab[step, 1] = ux
            pslab[step, 2] = uy
            pslab[step, 3] = uz
            pslab[step, 4] = 0.5 / temper
            others(lambda s: spread(s).start())
            ag[step, me] = pslab[step]

        if n_vert <= owners:
            own()
        else:
            pl.when(me < owners)(own)
        others_owning(lambda o: from_owner(o).wait_recv())
        for o in range(owners):
            for p in range(5):
                par[p, SLAB * o : SLAB * (o + 1), :] = ag[step, o, p]
        others_owning(lambda o: to_owner(o).wait_send())
        if n_vert <= owners:
            others(lambda s: spread(s).wait_send())
        else:
            pl.when(me < owners)(lambda: others(lambda s: spread(s).wait_send()))

    def move_first(c):
        send(ys1, yh1, ys1_s, ys1_r, c, to_y).wait_recv()
        send(xs1, xh1, xs1_s, xs1_r, c, to_x).wait_recv()
        for up in (True, False):
            @pl.when(x_up if up else jnp.logical_not(x_up))
            def _():
                each(chunk_groups, lambda n: move_group(c * chunk_groups + n, up, xh1, yh1, xs2))
        send(xs2, xh2, xs2_s, xs2_r, c, to_x).start()

    acc[...] = jnp.zeros_like(acc)
    each(chunks, move_first)
    reduce_moments(0)

    keep = 1.0 - rate[...]
    ramp = rate[...] * par[0]
    for p, value in enumerate((keep, ramp, par[1], par[2], par[3], par[4])):
        two = jnp.where(x_up, value[rows - 2 : rows], value[0:2])
        for q in range(PAD // 2):
            hps[p, 2 * q : 2 * q + 2, :] = two
    edges = pltpu.make_async_remote_copy(
        src_ref=hps, dst_ref=hpr, send_sem=hp_s, recv_sem=hp_r, device_id=to_x, device_id_type=MESH)
    edges.start()

    def fill_ez(l):
        dz = speed_of(l) - par[3]
        ez[l] = jnp.exp(-par[4] * dz * dz)

    each(VG, fill_ez)

    def collide_chunk(c):
        def collide(n, z):
            g = c * chunk_groups + n
            i, j, l0 = group_place(first, g, size)
            turn = jnp.where(j >= HALF, 2 * NZ, 0)
            keep = 1.0 - rate[...]
            amp = amplitudes(rate[...] * par[0], par[1], par[2], par[4], speed_of(i), speed_of(j))
            packed = jnp.zeros((rows, cols), jnp.float32)
            for t in range(size):
                v = g * size + t
                f = keep * state[v, 0:rows, :] + amp * ez[l0 + t]
                state[v, 0:rows, :] = f
                packed = jnp.where(slot == t, pltpu.roll(f, 2 * NZ * t + turn, 1), packed)
            ys2[g] = packed
            return z

        lax.fori_loop(0, chunk_groups, collide, 0)
        send(ys2, yh2, ys2_s, ys2_r, c, to_y).start()

    each(chunks, collide_chunk)

    edges.wait_recv()
    packed_rows = xh2.shape[1]
    for s in range(VG // size):
        for q in range(packed_rows // PAD):
            index = s * size + (lax.broadcasted_iota(jnp.int32, (PAD, cols), 0) + PAD * q) // 2
            dz = speed_of(index) - hpr[4]
            ezh[s, PAD * q : PAD * (q + 1), :] = jnp.exp(-hpr[5] * dz * dz)

    def collide_edge(g):
        i, j, l0 = group_place(first, g, size)
        amp = amplitudes(hpr[1], hpr[2], hpr[3], hpr[5], speed_of(i), speed_of(j))
        for q in range(packed_rows // PAD):
            part = slice(PAD * q, PAD * (q + 1))
            xh2[g, part, :] = hpr[0] * xh2[g, part, :] + amp * ezh[l0 // size, part, :]

    def move_second(c):
        send(ys2, yh2, ys2_s, ys2_r, c, to_y).wait_recv()
        send(xs2, xh2, xs2_s, xs2_r, c, to_x).wait_recv()
        each(chunk_groups, lambda n: collide_edge(c * chunk_groups + n))
        for up in (True, False):
            @pl.when(x_up if up else jnp.logical_not(x_up))
            def _():
                each(chunk_groups, lambda n: move_group(c * chunk_groups + n, up, xh2, yh2, None))
        store(c).start()

    acc[...] = jnp.zeros_like(acc)
    each(chunks, move_second)
    reduce_moments(1)
    par_out[...] = par[...]

    def finish(c):
        store(c).wait()
        send(xs1, xh1, xs1_s, xs1_r, c, to_x).wait_send()
        send(xs2, xh2, xs2_s, xs2_r, c, to_x).wait_send()
        send(ys1, yh1, ys1_s, ys1_r, c, to_y).wait_send()
        send(ys2, yh2, ys2_s, ys2_r, c, to_y).wait_send()

    each(chunks, finish)
    edges.wait_send()


def stream_rows(n_vert, dist, rate, out, par_out, T, U, ys1, yh1, ys2, yh2, tab, acc, mom, rs, pslab, ag, par, ez, ey,
                amp, hps, hpr, weights, load_sem, out_sem, xs1_s, xs1_r, xs2_s, xs2_r, ys1_s, ys1_r, ys2_s, ys2_r,
                rs_s, rs_r, ag_s, ag_r, hp_s, hp_r):
    count, rows, cols = dist.shape
    chunks = count // CHUNK
    per_chunk = CHUNK // SUB
    gx, gy, me = lax.axis_index("gx"), lax.axis_index("gy"), lax.axis_index("vert")
    to_x = {"gx": 1 - gx}
    to_y = {"gy": 1 - gy}
    first = me * count
    x_up = me * 2 >= n_vert
    sign = jnp.where(x_up, 1, -1)
    start = jnp.where(x_up, 2, rows + 1)
    edge_from = jnp.where(x_up, rows, 2)
    edge_to = jnp.where(x_up, 0, rows + 2)
    lane = lax.broadcasted_iota(jnp.int32, (SUB, cols), 1)
    sub = lax.broadcasted_iota(jnp.int32, (SUB, cols), 0)
    slot = lane // (2 * NZ)

    def row(k):
        return start + sign * k

    def each(n, fn, low=0):
        lax.fori_loop(low, n, lambda c, z: (fn(c), z)[1], 0)

    def span(c):
        return pl.ds(c * CHUNK, CHUNK)

    def load_start(c):
        each(rows, lambda x: pltpu.make_async_copy(
            dist.at[span(c), x, :], T.at[x + 2, span(c), :], load_sem.at[c]).start())

    def load_wait(c):
        inner = (pl.ds(2, rows), span(c))
        pltpu.make_async_copy(U.at[inner], T.at[inner], load_sem.at[c]).wait()

    def store_start(c):
        each(rows, lambda x: pltpu.make_async_copy(
            U.at[x + 2, span(c), :], out.at[span(c), x, :], out_sem.at[c]).start())

    def store_wait(c):
        inner = (pl.ds(2, rows), span(c))
        pltpu.make_async_copy(U.at[inner], T.at[inner], out_sem.at[c]).wait()

    def send_x(buf, s_sem, r_sem, c):
        return pltpu.make_async_remote_copy(
            src_ref=buf.at[pl.ds(edge_from, 2), span(c)], dst_ref=buf.at[pl.ds(edge_to, 2), span(c)],
            send_sem=s_sem.at[c], recv_sem=r_sem.at[c], device_id=to_x, device_id_type=MESH)

    def send_first(n):
        c, side = n // 2, lax.rem(n, 2)
        return pltpu.make_async_remote_copy(
            src_ref=dist.at[span(c), edge_from - 2 + side, :], dst_ref=T.at[edge_to + side, span(c), :],
            send_sem=xs1_s.at[n], recv_sem=xs1_r.at[n], device_id=to_x, device_id_type=MESH)

    def send_y(src, dst, s_sem, r_sem, c):
        part = pl.ds(c * per_chunk, per_chunk)
        return pltpu.make_async_remote_copy(
            src_ref=src.at[part], dst_ref=dst.at[part], send_sem=s_sem.at[c], recv_sem=r_sem.at[c],
            device_id=to_y, device_id_type=MESH)

    def chunk_place(c):
        begin = first + c * CHUNK
        return begin // (VG * VG), lax.rem(begin // CHUNK, 2)

    def by_half(half, fn):
        for up in (True, False):
            pl.when(half == (1 if up else 0))(functools.partial(fn, up))

    each(chunks, load_start)

    barrier = pltpu.get_barrier_semaphore()
    pl.semaphore_signal(barrier, inc=1, device_id=to_x, device_id_type=MESH)
    pl.semaphore_signal(barrier, inc=1, device_id=to_y, device_id_type=MESH)
    each(n_vert, lambda k: pl.semaphore_signal(
        barrier, inc=1, device_id={"vert": lax.rem(me + k, n_vert)}, device_id_type=MESH), 1)

    def fill_table(g):
        spot = (g * SUB + sub).astype(jnp.float32)
        j = jnp.floor((spot + 0.5) * (1.0 / VG))
        cy = STEP * (j + 0.5) - SPEED_MAX
        cz = STEP * (spot - VG * j + 0.5) - SPEED_MAX
        ay, az = DT * jnp.abs(cy), DT * jnp.abs(cz)
        tab[g, 0] = 1.0 - 1.5 * ay - 2.0 * az
        tab[g, 1] = 2.0 * ay
        tab[g, 2] = 2.0 * az
        tab[g, 3] = cy
        tab[g, 4] = cz
        tab[g, 5] = cy * cy + cz * cz

    each(2 * per_chunk, fill_table)

    def fill_weights():
        source = lax.broadcasted_iota(jnp.int32, (cols, cols), 0)
        target = lax.broadcasted_iota(jnp.int32, (cols, cols), 1)
        swap = jnp.where(source == target + 1 - 2 * (target % NZ), 1.0, 0.0).astype(jnp.bfloat16)
        for half, step in ((0, NZ), (1, -NZ)):
            along = jnp.where(source == target + step, 1.0, jnp.where(source == target + 2 * step, -0.25, 0.0))
            for part in range(2):
                at = slice(part * cols, (part + 1) * cols)
                weights[half, at, 0:cols] = along.astype(jnp.bfloat16)
                weights[half, at, cols : 2 * cols] = swap

    fill_weights()
    pl.semaphore_wait(barrier, n_vert + 1)
    each(2 * chunks, lambda n: send_first(n).start())

    def pack_chunk(c):
        load_wait(c)
        _, half = chunk_place(c)

        def run(up):
            def pack(n):
                at = pl.ds(pl.multiple_of(c * CHUNK + n * SUB, SUB), SUB)
                packed = jnp.zeros((SUB, cols), jnp.float32)
                for k in range(rows):
                    turned = pltpu.roll(T[row(k), at, :], (2 * NZ * k + (2 * NZ if up else 0)) % cols, 1)
                    packed = jnp.where(slot == k, turned, packed)
                ys1[c * per_chunk + n] = packed

            each(per_chunk, pack)

        by_half(half, run)
        send_y(ys1, yh1, ys1_s, ys1_r, c).start()

    each(chunks, pack_chunk)

    def move_chunk(c, yh):
        i, half = chunk_place(c)
        cx = speed_of(i)
        ax = DT * jnp.abs(cx)

        def run(up):
            outer = 0 if up else cols - 2 * NZ
            in_edge = lane < 2 * NZ if up else lane >= outer
            inside = lane % (2 * NZ)

            def from_edges(g):
                halo = yh[g]
                if up:
                    return jnp.where(inside < NZ, pltpu.roll(halo, cols - NZ, 1), 0.0) - 0.25 * halo
                return jnp.where(inside >= NZ, pltpu.roll(halo, NZ, 1), 0.0) - 0.25 * halo

            def block(kb):
                k0 = kb * BLOCK

                def five(sb, sums):
                    sums = list(sums)
                    at = pl.ds(pl.multiple_of(c * CHUNK + sb * 5 * SUB, SUB), 5 * SUB)
                    f = [T[row(k0 + kk), at, :] for kk in range(-2, BLOCK)]
                    mid = jnp.concatenate(f[2:], axis=0)
                    high = mid.astype(jnp.bfloat16)
                    low = (mid - high.astype(jnp.float32)).astype(jnp.bfloat16)
                    mixed = jnp.dot(jnp.concatenate([high, low], axis=1), weights[1 if up else 0],
                                    preferred_element_type=jnp.float32)
                    for q in range(5):
                        n = sb * 5 + q
                        at = pl.ds(pl.multiple_of(c * CHUNK + n * SUB, SUB), SUB)
                        place = half * per_chunk + n
                        c0 = tab[place, 0] - 1.5 * ax
                        by, bz = tab[place, 1], tab[place, 2]
                        cy, cz, cq = tab[place, 3], tab[place, 4], tab[place, 5]
                        terms = from_edges(c * per_chunk + n)
                        own = slice(q * SUB, (q + 1) * SUB)
                        for kk in range(BLOCK):
                            far_x, near_x, here = f[kk][own], f[kk + 1][own], f[kk + 2][own]
                            back = lax.rem(outer + cols - 2 * NZ * (k0 + kk), cols)
                            edge = jnp.where(in_edge, pltpu.roll(terms, back, 1), 0.0)
                            got = slice((kk * 5 + q) * SUB, (kk * 5 + q + 1) * SUB)
                            m = (c0 * here + (2.0 * ax) * (near_x - 0.25 * far_x)) + (
                                by * (mixed[got, 0:cols] + edge) + bz * mixed[got, cols : 2 * cols])
                            U[row(k0 + kk), at, :] = m
                            sums[4 * kk] = sums[4 * kk] + m
                            sums[4 * kk + 1] = sums[4 * kk + 1] + cy * m
                            sums[4 * kk + 2] = sums[4 * kk + 2] + cz * m
                            sums[4 * kk + 3] = sums[4 * kk + 3] + cq * m
                    return tuple(sums)

                zero = jnp.zeros((SUB, cols), jnp.float32)
                sums = lax.fori_loop(0, per_chunk // 5, five, (zero,) * (4 * BLOCK))
                for kk in range(BLOCK):
                    x = row(k0 + kk) - 2
                    a, my, mz, mq = sums[4 * kk : 4 * kk + 4]
                    acc[0, x] += a
                    acc[1, x] += cx * a
                    acc[2, x] += my
                    acc[3, x] += mz
                    acc[4, x] += (cx * cx) * a + mq

            each(rows // BLOCK, block)

        by_half(half, run)

    def reduce_moments(step):
        for o in range(n_vert):
            for p in range(5):
                mom[o, p] = jnp.sum(acc[p, SLAB * o : SLAB * (o + 1)], axis=1)

        def to_owner(o):
            return pltpu.make_async_remote_copy(
                src_ref=mom.at[o], dst_ref=rs.at[step, me], send_sem=rs_s.at[step, o], recv_sem=rs_r.at[step, me],
                device_id={"vert": o}, device_id_type=MESH)

        def from_device(s):
            return pltpu.make_async_remote_copy(
                src_ref=mom.at[s], dst_ref=rs.at[step, s], send_sem=rs_s.at[step, s], recv_sem=rs_r.at[step, s],
                device_id={"vert": s}, device_id_type=MESH)

        def spread(s):
            return pltpu.make_async_remote_copy(
                src_ref=pslab.at[step], dst_ref=ag.at[step, me], send_sem=ag_s.at[step, s],
                recv_sem=ag_r.at[step, me], device_id={"vert": s}, device_id_type=MESH)

        def from_owner(o):
            return pltpu.make_async_remote_copy(
                src_ref=pslab.at[step], dst_ref=ag.at[step, o], send_sem=ag_s.at[step, o],
                recv_sem=ag_r.at[step, o], device_id={"vert": o}, device_id_type=MESH)

        def others(fn):
            each(n_vert, lambda k: fn(lax.rem(me + k, n_vert)), 1)

        others(lambda o: to_owner(o).start())
        others(lambda s: from_device(s).wait_recv())
        total = lax.fori_loop(1, n_vert, lambda k, t: t + rs[step, lax.rem(me + k, n_vert)], mom[me])
        mass = total[0]
        ux, uy, uz = total[1] / mass, total[2] / mass, total[3] / mass
        temper = (total[4] / mass - (ux * ux + uy * uy + uz * uz)) / 3.0
        pslab[step, 0] = WEIGHT * mass / (temper * jnp.sqrt(temper))
        pslab[step, 1] = ux
        pslab[step, 2] = uy
        pslab[step, 3] = uz
        pslab[step, 4] = 0.5 / temper
        others(lambda s: spread(s).start())
        ag[step, me] = pslab[step]
        others(lambda o: from_owner(o).wait_recv())
        others(lambda o: to_owner(o).wait_send())
        others(lambda s: spread(s).wait_send())

    def move_first(c):
        send_y(ys1, yh1, ys1_s, ys1_r, c).wait_recv()
        send_first(2 * c).wait_recv()
        send_first(2 * c + 1).wait_recv()
        move_chunk(c, yh1)
        send_x(U, xs2_s, xs2_r, c).start()

    acc[...] = jnp.zeros_like(acc)
    each(chunks, move_first)
    reduce_moments(0)

    par[...] = jnp.ones_like(par)
    par[0, 2 : rows + 2, :] = 1.0 - rate[...]
    for o in range(n_vert):
        at = slice(SLAB * o + 2, SLAB * (o + 1) + 2)
        par[1, at, :] = rate[SLAB * o : SLAB * (o + 1), :] * ag[0, o, 0]
        for p in range(1, 5):
            par[p + 1, at, :] = ag[0, o, p]
    for p in range(6):
        hps[p] = jnp.where(x_up, par[p, rows : rows + 2, :], par[p, 2:4, :])
    edges = pltpu.make_async_remote_copy(
        src_ref=hps, dst_ref=hpr, send_sem=hp_s, recv_sem=hp_r, device_id=to_x, device_id_type=MESH)
    edges.start()

    def fill_ey():
        def one(j):
            dy = speed_of(j) - par[3]
            ey[j] = jnp.exp(-par[5] * dy * dy)
        each(VG, one)

    def fill_ez(r):
        for q in range(5):
            dz = tab[q, 4] - par[4, pl.ds(r, 1), :]
            ez[q, r] = jnp.exp(-par[5, pl.ds(r, 1), :] * dz * dz)

    def fill_amp(c):
        i, half = chunk_place(c)
        dx = speed_of(i) - par[2]
        front = par[1] * jnp.exp(-par[5] * dx * dx)
        for j in range(VG // 2):
            amp[j] = front * ey[half * (VG // 2) + j]

    def collided(c, sb, r):
        low = jnp.broadcast_to(amp[2 * sb, pl.ds(r, 1), :], (SUB, cols))
        high = jnp.broadcast_to(amp[2 * sb + 1, pl.ds(r, 1), :], (SUB, cols))
        keep = jnp.broadcast_to(par[0, pl.ds(r, 1), :], (SUB, cols))
        mixed = jnp.where(sub < SUB // 2, low, high)
        found = []
        for q, front in enumerate((low, low, mixed, high, high)):
            at = pl.ds(pl.multiple_of(c * CHUNK + (sb * 5 + q) * SUB, SUB), SUB)
            f = keep * U[r, at, :] + front * ez[q, r]
            T[r, at, :] = f
            found.append(f)
        return found

    fill_ey()
    each(rows, lambda x: fill_ez(x + 2))

    def collide_chunk(c):
        _, half = chunk_place(c)
        fill_amp(c)

        def run(up):
            def five(sb):
                def some(kb, packed):
                    packed = list(packed)
                    for kk in range(BLOCK):
                        k = kb * BLOCK + kk
                        turn = lax.rem(2 * NZ * k + (2 * NZ if up else 0), cols)
                        here = slot == k
                        for q, f in enumerate(collided(c, sb, row(k))):
                            packed[q] = jnp.where(here, pltpu.roll(f, turn, 1), packed[q])
                    return tuple(packed)

                zero = jnp.zeros((SUB, cols), jnp.float32)
                packed = lax.fori_loop(0, rows // BLOCK, some, (zero,) * 5)
                for q in range(5):
                    ys2[c * per_chunk + sb * 5 + q] = packed[q]

            each(per_chunk // 5, five)

        by_half(half, run)
        send_y(ys2, yh2, ys2_s, ys2_r, c).start()

    each(chunks, collide_chunk)

    edges.wait_recv()
    for p in range(6):
        par[p, 0:2, :] = hpr[p]
        par[p, rows + 2 : rows + 4, :] = hpr[p]
    fill_ey()
    each(2, lambda x: fill_ez(edge_to + x))

    def move_second(c):
        send_y(ys2, yh2, ys2_s, ys2_r, c).wait_recv()
        send_x(U, xs2_s, xs2_r, c).wait_recv()
        send_x(U, xs2_s, xs2_r, c).wait_send()
        fill_amp(c)

        def edge(sb):
            collided(c, sb, edge_to)
            collided(c, sb, edge_to + 1)

        each(per_chunk // 5, edge)
        move_chunk(c, yh2)
        store_start(c)

    acc[...] = jnp.zeros_like(acc)
    each(chunks, move_second)
    reduce_moments(1)
    for o in range(n_vert):
        for p in range(5):
            par_out[p, SLAB * o : SLAB * (o + 1), :] = ag[1, o, p]

    def finish(c):
        store_wait(c)
        send_y(ys1, yh1, ys1_s, ys1_r, c).wait_send()
        send_y(ys2, yh2, ys2_s, ys2_r, c).wait_send()

    each(chunks, finish)
    each(2 * chunks, lambda n: send_first(n).wait_send())
    edges.wait_send()


def run_rows(n_vert, distribution, collision_rate):
    count, rows, cols = distribution.shape
    chunks, groups = count // CHUNK, count // SUB
    f32 = jnp.float32
    state = pltpu.VMEM((rows + 4, count, cols), f32)
    y_edge = pltpu.VMEM((groups, SUB, cols), f32)
    dma = pltpu.SemaphoreType.DMA
    vmem = pl.BlockSpec(memory_space=pltpu.VMEM)
    anywhere = pl.BlockSpec(memory_space=pl.ANY)
    return pl.pallas_call(
        functools.partial(stream_rows, n_vert),
        out_shape=(jax.ShapeDtypeStruct(distribution.shape, f32), jax.ShapeDtypeStruct((5, rows, cols), f32)),
        in_specs=[anywhere, vmem],
        out_specs=(anywhere, vmem),
        scratch_shapes=[
            state, state, y_edge, y_edge, y_edge, y_edge,
            pltpu.VMEM((2 * CHUNK // SUB, 6, SUB, cols), f32),
            pltpu.VMEM((5, rows, SUB, cols), f32),
            pltpu.VMEM((n_vert, 5, SLAB, cols), f32),
            pltpu.VMEM((2, n_vert, 5, SLAB, cols), f32),
            pltpu.VMEM((2, 5, SLAB, cols), f32),
            pltpu.VMEM((2, n_vert, 5, SLAB, cols), f32),
            pltpu.VMEM((6, rows + 4, cols), f32),
            pltpu.VMEM((5, rows + 4, SUB, cols), f32),
            pltpu.VMEM((VG, rows + 4, cols), f32),
            pltpu.VMEM((VG // 2, rows + 4, cols), f32),
            pltpu.VMEM((6, 2, cols), f32),
            pltpu.VMEM((6, 2, cols), f32),
            pltpu.VMEM((2, 2 * cols, 2 * cols), jnp.bfloat16),
        ]
        + [dma((chunks,))] * 2 + [dma((2 * chunks,))] * 2 + [dma((chunks,))] * 6
        + [dma((2, n_vert))] * 4 + [dma, dma],
        compiler_params=pltpu.CompilerParams(
            collective_id=1, has_side_effects=True, vmem_limit_bytes=56 * 1024 * 1024),
        name="stream_rows",
    )(distribution, collision_rate)


def relax(size, chunk_groups, moved, rate, par, out, ez):
    step = pl.program_id(0)
    first = lax.axis_index("vert") * (pl.num_programs(0) * chunk_groups * size)

    @pl.when(step == 0)
    def _():
        def fill(l, z):
            dz = speed_of(l) - par[3]
            ez[l] = jnp.exp(-par[4] * dz * dz)
            return z
        lax.fori_loop(0, VG, fill, 0)

    keep = 1.0 - rate[...]
    for n in range(chunk_groups):
        i, j, l0 = group_place(first, step * chunk_groups + n, size)
        amp = amplitudes(rate[...] * par[0], par[1], par[2], par[4], speed_of(i), speed_of(j))
        for t in range(size):
            out[n * size + t] = keep * moved[n * size + t] + amp * ez[l0 + t]


def body(mesh, distribution, collision_rate):
    count, rows, cols = distribution.shape
    n_vert = mesh.shape["vert"]
    size = math.gcd(count, VG)
    groups = count // size
    chunk_groups = math.gcd(groups, 5)
    chunks = groups // chunk_groups
    packed_rows = -(-2 * size // PAD) * PAD
    owners = rows // SLAB
    f32 = jnp.float32
    x_edge = pltpu.VMEM((groups, packed_rows, cols), f32)
    y_edge = pltpu.VMEM((groups, rows, cols), f32)
    dma = pltpu.SemaphoreType.DMA
    vmem = pl.BlockSpec(memory_space=pltpu.VMEM)
    anywhere = pl.BlockSpec(memory_space=pl.ANY)
    if count % CHUNK == 0 and rows == SLAB * n_vert:
        moved, par = run_rows(n_vert, distribution, collision_rate)
    else:
        moved, par = pl.pallas_call(
            functools.partial(stream, n_vert, size, chunk_groups),
            out_shape=(jax.ShapeDtypeStruct(distribution.shape, f32), jax.ShapeDtypeStruct((5, rows, cols), f32)),
            in_specs=[anywhere, vmem],
            out_specs=(anywhere, vmem),
            scratch_shapes=[
                pltpu.VMEM((count, rows + PAD, cols), f32),
                x_edge, x_edge, x_edge, x_edge,
                y_edge, y_edge, y_edge, y_edge,
                pltpu.VMEM((5, rows, cols), f32),
                pltpu.VMEM((owners, 5, SLAB, cols), f32),
                pltpu.VMEM((2, n_vert, 5, SLAB, cols), f32),
                pltpu.VMEM((2, 5, SLAB, cols), f32),
                pltpu.VMEM((2, owners, 5, SLAB, cols), f32),
                pltpu.VMEM((5, rows, cols), f32),
                pltpu.VMEM((VG, rows, cols), f32),
                pltpu.VMEM((6, PAD, cols), f32),
                pltpu.VMEM((6, PAD, cols), f32),
                pltpu.VMEM((VG // size, packed_rows, cols), f32),
            ]
            + [dma((chunks,))] * 10
            + [dma((2, owners)), dma((2, n_vert)), dma((2, n_vert)), dma((2, owners)), dma, dma],
            compiler_params=pltpu.CompilerParams(
                collective_id=0, has_side_effects=True, vmem_limit_bytes=56 * 1024 * 1024),
            name="stream",
        )(distribution, collision_rate)
    block = pl.BlockSpec((chunk_groups * size, rows, cols), lambda c: (c, 0, 0))
    return pl.pallas_call(
        functools.partial(relax, size, chunk_groups),
        out_shape=jax.ShapeDtypeStruct(distribution.shape, f32),
        grid=(chunks,),
        in_specs=[block, vmem, vmem],
        out_specs=block,
        scratch_shapes=[pltpu.VMEM((VG, rows, cols), f32)],
        compiler_params=pltpu.CompilerParams(vmem_limit_bytes=60 * 1024 * 1024),
        name="relax",
    )(moved, collision_rate, par)


def solution(mesh):
    placed = (P("vert", "gx", "gy"), P("gx", "gy"))
    return jax.shard_map(
        functools.partial(body, mesh), mesh=mesh, in_specs=placed, out_specs=P("vert", "gx", "gy"), check_vma=False)
```

```python
import functools
import math

import jax
import jax.numpy as jnp
from jax import lax
from jax.experimental import pallas as pl
from jax.experimental.pallas import tpu as pltpu
from jax.sharding import PartitionSpec as P

VG = 20
NZ = 2
SPEED_MAX = 4.5
DT = 0.3 / 4.5
STEP = 2.0 * SPEED_MAX / VG
WEIGHT = STEP**3 / (2.0 * math.pi) ** 1.5
MESH = pl.DeviceIdType.MESH
HALF = VG // 2
SLAB = 4
PAD = 8
SUB = 8
CHUNK = VG * VG // 2
BLOCK = 4


def speed_of(index):
    if isinstance(index, int):
        return STEP * (index + 0.5) - SPEED_MAX
    return STEP * (index.astype(jnp.float32) + 0.5) - SPEED_MAX


def group_place(first, group, size):
    start = first + group * size
    last = 0 if size == VG else lax.rem(start, VG)
    return start // (VG * VG), lax.rem(start // VG, VG), last


def amplitudes(ramp, flow_x, flow_y, inv, cx, cy):
    dx = cx - flow_x
    dy = cy - flow_y
    return ramp * jnp.exp(-inv * (dx * dx + dy * dy))


def stream(n_vert, size, chunk_groups, dist, rate, out, par_out, state, xs1, xh1, xs2, xh2, ys1, yh1, ys2, yh2,
           acc, mom, rs, pslab, ag, par, ez, hps, hpr, ezh, load_sem, out_sem,
           xs1_s, xs1_r, xs2_s, xs2_r, ys1_s, ys1_r, ys2_s, ys2_r, rs_s, rs_r, ag_s, ag_r, hp_s, hp_r):
    count, rows, cols = dist.shape
    groups = count // size
    chunks = groups // chunk_groups
    chunk_vel = chunk_groups * size
    owners = rows // SLAB
    gx, gy, me = lax.axis_index("gx"), lax.axis_index("gy"), lax.axis_index("vert")
    to_x = {"gx": 1 - gx}
    to_y = {"gy": 1 - gy}
    first = me * count
    x_up = me * 2 >= n_vert
    lane = lax.broadcasted_iota(jnp.int32, (rows, cols), 1)
    even = lane % NZ == 0
    slot = lane // (2 * NZ)

    def load(c):
        part = pl.ds(c * chunk_vel, chunk_vel)
        return pltpu.make_async_copy(dist.at[part], state.at[part, pl.ds(0, rows)], load_sem.at[c])

    def store(c):
        part = pl.ds(c * chunk_vel, chunk_vel)
        return pltpu.make_async_copy(state.at[part, pl.ds(0, rows)], out.at[part], out_sem.at[c])

    def send(src, dst, s_sem, r_sem, c, device):
        part = pl.ds(c * chunk_groups, chunk_groups)
        return pltpu.make_async_remote_copy(
            src_ref=src.at[part], dst_ref=dst.at[part], send_sem=s_sem.at[c], recv_sem=r_sem.at[c],
            device_id=device, device_id_type=MESH)

    def each(n, fn, low=0):
        lax.fori_loop(low, n, lambda c, z: (fn(c), z)[1], 0)

    each(chunks, lambda c: load(c).start())

    barrier = pltpu.get_barrier_semaphore()
    pl.semaphore_signal(barrier, inc=1, device_id=to_x, device_id_type=MESH)
    pl.semaphore_signal(barrier, inc=1, device_id=to_y, device_id_type=MESH)
    each(n_vert, lambda k: pl.semaphore_signal(
        barrier, inc=1, device_id={"vert": lax.rem(me + k, n_vert)}, device_id_type=MESH), 1)
    pl.semaphore_wait(barrier, n_vert + 1)

    def pack_chunk(c):
        load(c).wait()

        def pack(n, z):
            g = c * chunk_groups + n
            _, j, _ = group_place(first, g, size)
            turn = jnp.where(j >= HALF, 2 * NZ, 0)
            packed = jnp.zeros((rows, cols), jnp.float32)
            for t in range(size):
                v = g * size + t
                f = state[v, 0:rows, :]
                packed = jnp.where(slot == t, pltpu.roll(f, 2 * NZ * t + turn, 1), packed)
                xs1[g, 2 * t : 2 * t + 2, :] = jnp.where(x_up, f[rows - 2 : rows], f[0:2])
            ys1[g] = packed
            return z

        lax.fori_loop(0, chunk_groups, pack, 0)
        send(xs1, xh1, xs1_s, xs1_r, c, to_x).start()
        send(ys1, yh1, ys1_s, ys1_r, c, to_y).start()

    each(chunks, pack_chunk)

    def move_group(g, up, xh, yh, xs):
        i, j, l0 = group_place(first, g, size)
        cx, cy = speed_of(i), speed_of(j)
        ax, ay = DT * jnp.abs(cx), DT * jnp.abs(cy)
        y_up = j >= HALF
        turn = jnp.where(y_up, 2 * NZ, 0)
        near = jnp.where(y_up, NZ, cols - NZ)
        far = jnp.where(y_up, 2 * NZ, cols - 2 * NZ)
        edge = lax.rem(lane + turn, cols)
        edge_near = jnp.where(y_up, edge - NZ, edge)
        in_far = edge < 2 * NZ
        in_near = (edge_near >= 0) & (edge_near < NZ)
        base = 1.0 - 1.5 * ax - 1.5 * ay
        halo = yh[g]
        a = b = d = jnp.zeros((rows, cols), jnp.float32)
        tall = rows + PAD
        at = tall - 2 if up else rows
        for t in range(size):
            v = g * size + t
            state[v, at : at + 2, :] = xh[g, 2 * t : 2 * t + 2, :]
        for t in range(size):
            v = g * size + t
            az = 2.0 * DT * (abs(speed_of(t)) if size == VG else jnp.abs(speed_of(l0 + t)))
            whole = state[v]
            f = whole[0:rows]
            near_x = pltpu.roll(whole, 1 if up else tall - 1, 0)[0:rows]
            far_x = pltpu.roll(whole, 2 if up else tall - 2, 0)[0:rows]
            other = jnp.where(even, pltpu.roll(f, cols - 1, 1), pltpu.roll(f, 1, 1))
            edge_f = pltpu.roll(halo, lax.rem(2 * cols - 2 * NZ * t - turn, cols), 1)
            near_y = pltpu.roll(jnp.where(in_near, edge_f, f), near, 1)
            far_y = pltpu.roll(jnp.where(in_far, edge_f, f), far, 1)
            m = (base - az) * f + (2.0 * ax) * near_x - (0.5 * ax) * far_x
            m = m + ((2.0 * ay) * near_y - (0.5 * ay) * far_y + az * other)
            state[v, 0:rows, :] = m
            if xs is not None:
                xs[g, 2 * t : 2 * t + 2, :] = m[rows - 2 : rows] if up else m[0:2]
            a = a + m
            b = b + a
            d = d + b
        e = speed_of(l0) + STEP * size
        acc[0] += a
        acc[1] += cx * a
        acc[2] += cy * a
        acc[3] += e * a - STEP * b
        acc[4] += (cx * cx + cy * cy + e * e) * a - (2.0 * STEP * e + STEP * STEP) * b + (2.0 * STEP * STEP) * d

    def reduce_moments(step):
        for o in range(owners):
            for p in range(5):
                mom[o, p] = acc[p, SLAB * o : SLAB * (o + 1), :]

        def to_owner(o):
            return pltpu.make_async_remote_copy(
                src_ref=mom.at[o], dst_ref=rs.at[step, me], send_sem=rs_s.at[step, o], recv_sem=rs_r.at[step, me],
                device_id={"vert": o}, device_id_type=MESH)

        def from_device(s):
            return pltpu.make_async_remote_copy(
                src_ref=mom.at[0], dst_ref=rs.at[step, s], send_sem=rs_s.at[step, 0], recv_sem=rs_r.at[step, s],
                device_id={"vert": s}, device_id_type=MESH)

        def spread(s):
            return pltpu.make_async_remote_copy(
                src_ref=pslab.at[step], dst_ref=ag.at[step, me], send_sem=ag_s.at[step, s],
                recv_sem=ag_r.at[step, me], device_id={"vert": s}, device_id_type=MESH)

        def from_owner(o):
            return pltpu.make_async_remote_copy(
                src_ref=pslab.at[step], dst_ref=ag.at[step, o], send_sem=ag_s.at[step, 0],
                recv_sem=ag_r.at[step, o], device_id={"vert": o}, device_id_type=MESH)

        def others_owning(fn):
            def one(k):
                o = lax.rem(me + k, n_vert)
                if n_vert <= owners:
                    fn(o)
                else:
                    pl.when(o < owners)(lambda: fn(o))
            each(n_vert, one, 1)

        def others(fn):
            each(n_vert, lambda k: fn(lax.rem(me + k, n_vert)), 1)

        others_owning(lambda o: to_owner(o).start())

        def own():
            others(lambda s: from_device(s).wait_recv())

            def add(k, total):
                return total + rs[step, lax.rem(me + k, n_vert)]

            total = lax.fori_loop(1, n_vert, add, mom[me])
            mass = total[0]
            ux, uy, uz = total[1] / mass, total[2] / mass, total[3] / mass
            temper = (total[4] / mass - (ux * ux + uy * uy + uz * uz)) / 3.0
            pslab[step, 0] = WEIGHT * mass / (temper * jnp.sqrt(temper))
            pslab[step, 1] = ux
            pslab[step, 2] = uy
            pslab[step, 3] = uz
            pslab[step, 4] = 0.5 / temper
            others(lambda s: spread(s).start())
            ag[step, me] = pslab[step]

        if n_vert <= owners:
            own()
        else:
            pl.when(me < owners)(own)
        others_owning(lambda o: from_owner(o).wait_recv())
        for o in range(owners):
            for p in range(5):
                par[p, SLAB * o : SLAB * (o + 1), :] = ag[step, o, p]
        others_owning(lambda o: to_owner(o).wait_send())
        if n_vert <= owners:
            others(lambda s: spread(s).wait_send())
        else:
            pl.when(me < owners)(lambda: others(lambda s: spread(s).wait_send()))

    def move_first(c):
        send(ys1, yh1, ys1_s, ys1_r, c, to_y).wait_recv()
        send(xs1, xh1, xs1_s, xs1_r, c, to_x).wait_recv()
        for up in (True, False):
            @pl.when(x_up if up else jnp.logical_not(x_up))
            def _():
                each(chunk_groups, lambda n: move_group(c * chunk_groups + n, up, xh1, yh1, xs2))
        send(xs2, xh2, xs2_s, xs2_r, c, to_x).start()

    acc[...] = jnp.zeros_like(acc)
    each(chunks, move_first)
    reduce_moments(0)

    keep = 1.0 - rate[...]
    ramp = rate[...] * par[0]
    for p, value in enumerate((keep, ramp, par[1], par[2], par[3], par[4])):
        two = jnp.where(x_up, value[rows - 2 : rows], value[0:2])
        for q in range(PAD // 2):
            hps[p, 2 * q : 2 * q + 2, :] = two
    edges = pltpu.make_async_remote_copy(
        src_ref=hps, dst_ref=hpr, send_sem=hp_s, recv_sem=hp_r, device_id=to_x, device_id_type=MESH)
    edges.start()

    def fill_ez(l):
        dz = speed_of(l) - par[3]
        ez[l] = jnp.exp(-par[4] * dz * dz)

    each(VG, fill_ez)

    def collide_chunk(c):
        def collide(n, z):
            g = c * chunk_groups + n
            i, j, l0 = group_place(first, g, size)
            turn = jnp.where(j >= HALF, 2 * NZ, 0)
            keep = 1.0 - rate[...]
            amp = amplitudes(rate[...] * par[0], par[1], par[2], par[4], speed_of(i), speed_of(j))
            packed = jnp.zeros((rows, cols), jnp.float32)
            for t in range(size):
                v = g * size + t
                f = keep * state[v, 0:rows, :] + amp * ez[l0 + t]
                state[v, 0:rows, :] = f
                packed = jnp.where(slot == t, pltpu.roll(f, 2 * NZ * t + turn, 1), packed)
            ys2[g] = packed
            return z

        lax.fori_loop(0, chunk_groups, collide, 0)
        send(ys2, yh2, ys2_s, ys2_r, c, to_y).start()

    collide_chunk(0)

    edges.wait_recv()
    packed_rows = xh2.shape[1]
    for s in range(VG // size):
        for q in range(packed_rows // PAD):
            index = s * size + (lax.broadcasted_iota(jnp.int32, (PAD, cols), 0) + PAD * q) // 2
            dz = speed_of(index) - hpr[4]
            ezh[s, PAD * q : PAD * (q + 1), :] = jnp.exp(-hpr[5] * dz * dz)

    def collide_edge(g):
        i, j, l0 = group_place(first, g, size)
        amp = amplitudes(hpr[1], hpr[2], hpr[3], hpr[5], speed_of(i), speed_of(j))
        for q in range(packed_rows // PAD):
            part = slice(PAD * q, PAD * (q + 1))
            xh2[g, part, :] = hpr[0] * xh2[g, part, :] + amp * ezh[l0 // size, part, :]

    def move_second(c):
        send(ys2, yh2, ys2_s, ys2_r, c, to_y).wait_recv()
        send(xs2, xh2, xs2_s, xs2_r, c, to_x).wait_recv()
        each(chunk_groups, lambda n: collide_edge(c * chunk_groups + n))
        for up in (True, False):
            @pl.when(x_up if up else jnp.logical_not(x_up))
            def _():
                each(chunk_groups, lambda n: move_group(c * chunk_groups + n, up, xh2, yh2, None))
        store(c).start()

    acc[...] = jnp.zeros_like(acc)
    each(chunks, move_second)
    reduce_moments(1)
    par_out[...] = par[...]

    def finish(c):
        store(c).wait()
        send(xs1, xh1, xs1_s, xs1_r, c, to_x).wait_send()
        send(xs2, xh2, xs2_s, xs2_r, c, to_x).wait_send()
        send(ys1, yh1, ys1_s, ys1_r, c, to_y).wait_send()
        send(ys2, yh2, ys2_s, ys2_r, c, to_y).wait_send()

    each(chunks, finish)
    edges.wait_send()


def stream_rows(n_vert, dist, rate, out, par_out, T, U, ys1, yh1, ys2, yh2, tab, acc, mom, rs, pslab, ag, par, ez, ey,
                amp, hps, hpr, weights, load_sem, out_sem, xs1_s, xs1_r, xs2_s, xs2_r, ys1_s, ys1_r, ys2_s, ys2_r,
                rs_s, rs_r, ag_s, ag_r, hp_s, hp_r):
    count, rows, cols = dist.shape
    chunks = count // CHUNK
    per_chunk = CHUNK // SUB
    gx, gy, me = lax.axis_index("gx"), lax.axis_index("gy"), lax.axis_index("vert")
    to_x = {"gx": 1 - gx}
    to_y = {"gy": 1 - gy}
    first = me * count
    x_up = me * 2 >= n_vert
    sign = jnp.where(x_up, 1, -1)
    start = jnp.where(x_up, 2, rows + 1)
    edge_from = jnp.where(x_up, rows, 2)
    edge_to = jnp.where(x_up, 0, rows + 2)
    lane = lax.broadcasted_iota(jnp.int32, (SUB, cols), 1)
    sub = lax.broadcasted_iota(jnp.int32, (SUB, cols), 0)
    slot = lane // (2 * NZ)

    def row(k):
        return start + sign * k

    def each(n, fn, low=0):
        lax.fori_loop(low, n, lambda c, z: (fn(c), z)[1], 0)

    def span(c):
        return pl.ds(c * CHUNK, CHUNK)

    def load_start(c):
        each(rows, lambda x: pltpu.make_async_copy(
            dist.at[span(c), x, :], T.at[x + 2, span(c), :], load_sem.at[c]).start())

    def load_wait(c):
        inner = (pl.ds(2, rows), span(c))
        pltpu.make_async_copy(U.at[inner], T.at[inner], load_sem.at[c]).wait()

    def store_start(c):
        each(rows, lambda x: pltpu.make_async_copy(
            U.at[x + 2, span(c), :], out.at[span(c), x, :], out_sem.at[c]).start())

    def store_wait(c):
        inner = (pl.ds(2, rows), span(c))
        pltpu.make_async_copy(U.at[inner], T.at[inner], out_sem.at[c]).wait()

    def send_x(buf, s_sem, r_sem, c):
        return pltpu.make_async_remote_copy(
            src_ref=buf.at[pl.ds(edge_from, 2), span(c)], dst_ref=buf.at[pl.ds(edge_to, 2), span(c)],
            send_sem=s_sem.at[c], recv_sem=r_sem.at[c], device_id=to_x, device_id_type=MESH)

    def send_first(n):
        c, side = n // 2, lax.rem(n, 2)
        return pltpu.make_async_remote_copy(
            src_ref=dist.at[span(c), edge_from - 2 + side, :], dst_ref=T.at[edge_to + side, span(c), :],
            send_sem=xs1_s.at[n], recv_sem=xs1_r.at[n], device_id=to_x, device_id_type=MESH)

    def send_y(src, dst, s_sem, r_sem, c):
        part = pl.ds(c * per_chunk, per_chunk)
        return pltpu.make_async_remote_copy(
            src_ref=src.at[part], dst_ref=dst.at[part], send_sem=s_sem.at[c], recv_sem=r_sem.at[c],
            device_id=to_y, device_id_type=MESH)

    def chunk_place(c):
        begin = first + c * CHUNK
        return begin // (VG * VG), lax.rem(begin // CHUNK, 2)

    def by_half(half, fn):
        for up in (True, False):
            pl.when(half == (1 if up else 0))(functools.partial(fn, up))

    each(chunks, load_start)

    barrier = pltpu.get_barrier_semaphore()
    pl.semaphore_signal(barrier, inc=1, device_id=to_x, device_id_type=MESH)
    pl.semaphore_signal(barrier, inc=1, device_id=to_y, device_id_type=MESH)
    each(n_vert, lambda k: pl.semaphore_signal(
        barrier, inc=1, device_id={"vert": lax.rem(me + k, n_vert)}, device_id_type=MESH), 1)

    def fill_table(g):
        spot = (g * SUB + sub).astype(jnp.float32)
        j = jnp.floor((spot + 0.5) * (1.0 / VG))
        cy = STEP * (j + 0.5) - SPEED_MAX
        cz = STEP * (spot - VG * j + 0.5) - SPEED_MAX
        ay, az = DT * jnp.abs(cy), DT * jnp.abs(cz)
        tab[g, 0] = 1.0 - 1.5 * ay - 2.0 * az
        tab[g, 1] = 2.0 * ay
        tab[g, 2] = 2.0 * az
        tab[g, 3] = cy
        tab[g, 4] = cz
        tab[g, 5] = cy * cy + cz * cz

    each(2 * per_chunk, fill_table)

    def fill_weights():
        source = lax.broadcasted_iota(jnp.int32, (cols, cols), 0)
        target = lax.broadcasted_iota(jnp.int32, (cols, cols), 1)
        swap = jnp.where(source == target + 1 - 2 * (target % NZ), 1.0, 0.0).astype(jnp.bfloat16)
        for half, step in ((0, NZ), (1, -NZ)):
            along = jnp.where(source == target + step, 1.0, jnp.where(source == target + 2 * step, -0.25, 0.0))
            for part in range(2):
                at = slice(part * cols, (part + 1) * cols)
                weights[half, at, 0:cols] = along.astype(jnp.bfloat16)
                weights[half, at, cols : 2 * cols] = swap

    fill_weights()
    pl.semaphore_wait(barrier, n_vert + 1)
    each(2 * chunks, lambda n: send_first(n).start())

    def pack_chunk(c):
        load_wait(c)
        _, half = chunk_place(c)

        def run(up):
            def pack(n):
                at = pl.ds(pl.multiple_of(c * CHUNK + n * SUB, SUB), SUB)
                packed = jnp.zeros((SUB, cols), jnp.float32)
                for k in range(rows):
                    turned = pltpu.roll(T[row(k), at, :], (2 * NZ * k + (2 * NZ if up else 0)) % cols, 1)
                    packed = jnp.where(slot == k, turned, packed)
                ys1[c * per_chunk + n] = packed

            each(per_chunk, pack)

        by_half(half, run)
        send_y(ys1, yh1, ys1_s, ys1_r, c).start()

    def move_chunk(c, yh):
        i, half = chunk_place(c)
        cx = speed_of(i)
        ax = DT * jnp.abs(cx)

        def run(up):
            outer = 0 if up else cols - 2 * NZ
            in_edge = lane < 2 * NZ if up else lane >= outer
            inside = lane % (2 * NZ)

            def from_edges(g):
                halo = yh[g]
                if up:
                    return jnp.where(inside < NZ, pltpu.roll(halo, cols - NZ, 1), 0.0) - 0.25 * halo
                return jnp.where(inside >= NZ, pltpu.roll(halo, NZ, 1), 0.0) - 0.25 * halo

            def block(kb):
                k0 = kb * BLOCK

                f = [T[row(k0 + kk), span(c), :] for kk in range(-2, BLOCK)]
                mid = jnp.concatenate(f[2:], axis=0)
                high = mid.astype(jnp.bfloat16)
                low = (mid - high.astype(jnp.float32)).astype(jnp.bfloat16)
                mixed = jnp.dot(jnp.concatenate([high, low], axis=1), weights[1 if up else 0],
                                preferred_element_type=jnp.float32)
                sums = [jnp.zeros((SUB, cols), jnp.float32)] * (4 * BLOCK)
                for n in range(per_chunk):
                    at = pl.ds(pl.multiple_of(c * CHUNK + n * SUB, SUB), SUB)
                    place = half * per_chunk + n
                    c0 = tab[place, 0] - 1.5 * ax
                    by, bz = tab[place, 1], tab[place, 2]
                    cy, cz, cq = tab[place, 3], tab[place, 4], tab[place, 5]
                    terms = from_edges(c * per_chunk + n)
                    own = slice(n * SUB, (n + 1) * SUB)
                    for kk in range(BLOCK):
                        far_x, near_x, here = f[kk][own], f[kk + 1][own], f[kk + 2][own]
                        back = lax.rem(outer + cols - 2 * NZ * (k0 + kk), cols)
                        edge = jnp.where(in_edge, pltpu.roll(terms, back, 1), 0.0)
                        got = slice(kk * CHUNK + n * SUB, kk * CHUNK + (n + 1) * SUB)
                        m = (c0 * here + (2.0 * ax) * (near_x - 0.25 * far_x)) + (
                            by * (mixed[got, 0:cols] + edge) + bz * mixed[got, cols : 2 * cols])
                        U[row(k0 + kk), at, :] = m
                        sums[4 * kk] = sums[4 * kk] + m
                        sums[4 * kk + 1] = sums[4 * kk + 1] + cy * m
                        sums[4 * kk + 2] = sums[4 * kk + 2] + cz * m
                        sums[4 * kk + 3] = sums[4 * kk + 3] + cq * m
                for kk in range(BLOCK):
                    x = row(k0 + kk) - 2
                    a, my, mz, mq = sums[4 * kk : 4 * kk + 4]
                    acc[0, x] += a
                    acc[1, x] += cx * a
                    acc[2, x] += my
                    acc[3, x] += mz
                    acc[4, x] += (cx * cx) * a + mq

            each(rows // BLOCK, block)

        by_half(half, run)

    def reduce_moments(step):
        for o in range(n_vert):
            for p in range(5):
                mom[o, p] = jnp.sum(acc[p, SLAB * o : SLAB * (o + 1)], axis=1)

        def to_owner(o):
            return pltpu.make_async_remote_copy(
                src_ref=mom.at[o], dst_ref=rs.at[step, me], send_sem=rs_s.at[step, o], recv_sem=rs_r.at[step, me],
                device_id={"vert": o}, device_id_type=MESH)

        def from_device(s):
            return pltpu.make_async_remote_copy(
                src_ref=mom.at[s], dst_ref=rs.at[step, s], send_sem=rs_s.at[step, s], recv_sem=rs_r.at[step, s],
                device_id={"vert": s}, device_id_type=MESH)

        def spread(s):
            return pltpu.make_async_remote_copy(
                src_ref=pslab.at[step], dst_ref=ag.at[step, me], send_sem=ag_s.at[step, s],
                recv_sem=ag_r.at[step, me], device_id={"vert": s}, device_id_type=MESH)

        def from_owner(o):
            return pltpu.make_async_remote_copy(
                src_ref=pslab.at[step], dst_ref=ag.at[step, o], send_sem=ag_s.at[step, o],
                recv_sem=ag_r.at[step, o], device_id={"vert": o}, device_id_type=MESH)

        def others(fn):
            each(n_vert, lambda k: fn(lax.rem(me + k, n_vert)), 1)

        others(lambda o: to_owner(o).start())
        others(lambda s: from_device(s).wait_recv())
        total = lax.fori_loop(1, n_vert, lambda k, t: t + rs[step, lax.rem(me + k, n_vert)], mom[me])
        mass = total[0]
        ux, uy, uz = total[1] / mass, total[2] / mass, total[3] / mass
        temper = (total[4] / mass - (ux * ux + uy * uy + uz * uz)) / 3.0
        pslab[step, 0] = WEIGHT * mass / (temper * jnp.sqrt(temper))
        pslab[step, 1] = ux
        pslab[step, 2] = uy
        pslab[step, 3] = uz
        pslab[step, 4] = 0.5 / temper
        others(lambda s: spread(s).start())
        ag[step, me] = pslab[step]
        others(lambda o: from_owner(o).wait_recv())
        others(lambda o: to_owner(o).wait_send())
        others(lambda s: spread(s).wait_send())

    def move_first(c):
        pl.when(c + 1 < chunks)(lambda: pack_chunk(c + 1))
        send_y(ys1, yh1, ys1_s, ys1_r, c).wait_recv()
        send_first(2 * c).wait_recv()
        send_first(2 * c + 1).wait_recv()
        move_chunk(c, yh1)
        send_x(U, xs2_s, xs2_r, c).start()

    acc[...] = jnp.zeros_like(acc)
    pack_chunk(0)
    each(chunks, move_first)
    reduce_moments(0)

    par[...] = jnp.ones_like(par)
    par[0, 2 : rows + 2, :] = 1.0 - rate[...]
    for o in range(n_vert):
        at = slice(SLAB * o + 2, SLAB * (o + 1) + 2)
        par[1, at, :] = rate[SLAB * o : SLAB * (o + 1), :] * ag[0, o, 0]
        for p in range(1, 5):
            par[p + 1, at, :] = ag[0, o, p]
    for p in range(6):
        hps[p] = jnp.where(x_up, par[p, rows : rows + 2, :], par[p, 2:4, :])
    edges = pltpu.make_async_remote_copy(
        src_ref=hps, dst_ref=hpr, send_sem=hp_s, recv_sem=hp_r, device_id=to_x, device_id_type=MESH)
    edges.start()

    def fill_ey():
        def one(j):
            dy = speed_of(j) - par[3]
            ey[j] = jnp.exp(-par[5] * dy * dy)
        each(VG, one)

    def fill_ez(r):
        for q in range(5):
            dz = tab[q, 4] - par[4, pl.ds(r, 1), :]
            ez[q, r] = jnp.exp(-par[5, pl.ds(r, 1), :] * dz * dz)

    def fill_amp(c):
        i, half = chunk_place(c)
        dx = speed_of(i) - par[2]
        front = par[1] * jnp.exp(-par[5] * dx * dx)
        for j in range(VG // 2):
            amp[j] = front * ey[half * (VG // 2) + j]

    def collided(c, sb, r):
        low = jnp.broadcast_to(amp[2 * sb, pl.ds(r, 1), :], (SUB, cols))
        high = jnp.broadcast_to(amp[2 * sb + 1, pl.ds(r, 1), :], (SUB, cols))
        keep = jnp.broadcast_to(par[0, pl.ds(r, 1), :], (SUB, cols))
        mixed = jnp.where(sub < SUB // 2, low, high)
        found = []
        for q, front in enumerate((low, low, mixed, high, high)):
            at = pl.ds(pl.multiple_of(c * CHUNK + (sb * 5 + q) * SUB, SUB), SUB)
            f = keep * U[r, at, :] + front * ez[q, r]
            T[r, at, :] = f
            found.append(f)
        return found

    fill_ey()
    each(rows, lambda x: fill_ez(x + 2))

    def collide_chunk(c):
        _, half = chunk_place(c)
        fill_amp(c)

        def run(up):
            def five(sb):
                def some(kb, packed):
                    packed = list(packed)
                    for kk in range(2 * BLOCK):
                        k = kb * 2 * BLOCK + kk
                        turn = lax.rem(2 * NZ * k + (2 * NZ if up else 0), cols)
                        here = slot == k
                        for q, f in enumerate(collided(c, sb, row(k))):
                            packed[q] = jnp.where(here, pltpu.roll(f, turn, 1), packed[q])
                    return tuple(packed)

                zero = jnp.zeros((SUB, cols), jnp.float32)
                packed = lax.fori_loop(0, rows // (2 * BLOCK), some, (zero,) * 5)
                for q in range(5):
                    ys2[c * per_chunk + sb * 5 + q] = packed[q]

            each(per_chunk // 5, five)

        by_half(half, run)
        send_y(ys2, yh2, ys2_s, ys2_r, c).start()

    collide_chunk(0)

    edges.wait_recv()
    for p in range(6):
        par[p, 0:2, :] = hpr[p]
        par[p, rows + 2 : rows + 4, :] = hpr[p]
    fill_ey()
    each(2, lambda x: fill_ez(edge_to + x))

    def move_second(c):
        pl.when(c + 1 < chunks)(lambda: collide_chunk(c + 1))
        send_y(ys2, yh2, ys2_s, ys2_r, c).wait_recv()
        send_x(U, xs2_s, xs2_r, c).wait_recv()
        send_x(U, xs2_s, xs2_r, c).wait_send()
        fill_amp(c)

        def edge(sb):
            collided(c, sb, edge_to)
            collided(c, sb, edge_to + 1)

        each(per_chunk // 5, edge)
        move_chunk(c, yh2)
        store_start(c)

    acc[...] = jnp.zeros_like(acc)
    each(chunks, move_second)
    reduce_moments(1)
    for o in range(n_vert):
        for p in range(5):
            par_out[p, SLAB * o : SLAB * (o + 1), :] = ag[1, o, p]

    def finish(c):
        store_wait(c)
        send_y(ys1, yh1, ys1_s, ys1_r, c).wait_send()
        send_y(ys2, yh2, ys2_s, ys2_r, c).wait_send()

    each(chunks, finish)
    each(2 * chunks, lambda n: send_first(n).wait_send())
    edges.wait_send()


def run_rows(n_vert, distribution, collision_rate):
    count, rows, cols = distribution.shape
    chunks, groups = count // CHUNK, count // SUB
    f32 = jnp.float32
    state = pltpu.VMEM((rows + 4, count, cols), f32)
    y_edge = pltpu.VMEM((groups, SUB, cols), f32)
    dma = pltpu.SemaphoreType.DMA
    vmem = pl.BlockSpec(memory_space=pltpu.VMEM)
    anywhere = pl.BlockSpec(memory_space=pl.ANY)
    return pl.pallas_call(
        functools.partial(stream_rows, n_vert),
        out_shape=(jax.ShapeDtypeStruct(distribution.shape, f32), jax.ShapeDtypeStruct((5, rows, cols), f32)),
        in_specs=[anywhere, vmem],
        out_specs=(anywhere, vmem),
        scratch_shapes=[
            state, state, y_edge, y_edge, y_edge, y_edge,
            pltpu.VMEM((2 * CHUNK // SUB, 6, SUB, cols), f32),
            pltpu.VMEM((5, rows, SUB, cols), f32),
            pltpu.VMEM((n_vert, 5, SLAB, cols), f32),
            pltpu.VMEM((2, n_vert, 5, SLAB, cols), f32),
            pltpu.VMEM((2, 5, SLAB, cols), f32),
            pltpu.VMEM((2, n_vert, 5, SLAB, cols), f32),
            pltpu.VMEM((6, rows + 4, cols), f32),
            pltpu.VMEM((5, rows + 4, SUB, cols), f32),
            pltpu.VMEM((VG, rows + 4, cols), f32),
            pltpu.VMEM((VG // 2, rows + 4, cols), f32),
            pltpu.VMEM((6, 2, cols), f32),
            pltpu.VMEM((6, 2, cols), f32),
            pltpu.VMEM((2, 2 * cols, 2 * cols), jnp.bfloat16),
        ]
        + [dma((chunks,))] * 2 + [dma((2 * chunks,))] * 2 + [dma((chunks,))] * 6
        + [dma((2, n_vert))] * 4 + [dma, dma],
        compiler_params=pltpu.CompilerParams(
            collective_id=1, has_side_effects=True, vmem_limit_bytes=56 * 1024 * 1024),
        name="stream_rows",
    )(distribution, collision_rate)


def relax(size, chunk_groups, moved, rate, par, out, ez):
    step = pl.program_id(0)
    first = lax.axis_index("vert") * (pl.num_programs(0) * chunk_groups * size)

    @pl.when(step == 0)
    def _():
        def fill(l, z):
            dz = speed_of(l) - par[3]
            ez[l] = jnp.exp(-par[4] * dz * dz)
            return z
        lax.fori_loop(0, VG, fill, 0)

    keep = 1.0 - rate[...]
    for n in range(chunk_groups):
        i, j, l0 = group_place(first, step * chunk_groups + n, size)
        amp = amplitudes(rate[...] * par[0], par[1], par[2], par[4], speed_of(i), speed_of(j))
        for t in range(size):
            out[n * size + t] = keep * moved[n * size + t] + amp * ez[l0 + t]


def body(mesh, distribution, collision_rate):
    count, rows, cols = distribution.shape
    n_vert = mesh.shape["vert"]
    size = math.gcd(count, VG)
    groups = count // size
    chunk_groups = math.gcd(groups, 5)
    chunks = groups // chunk_groups
    packed_rows = -(-2 * size // PAD) * PAD
    owners = rows // SLAB
    f32 = jnp.float32
    x_edge = pltpu.VMEM((groups, packed_rows, cols), f32)
    y_edge = pltpu.VMEM((groups, rows, cols), f32)
    dma = pltpu.SemaphoreType.DMA
    vmem = pl.BlockSpec(memory_space=pltpu.VMEM)
    anywhere = pl.BlockSpec(memory_space=pl.ANY)
    if count % CHUNK == 0 and rows == SLAB * n_vert:
        moved, par = run_rows(n_vert, distribution, collision_rate)
    else:
        moved, par = pl.pallas_call(
            functools.partial(stream, n_vert, size, chunk_groups),
            out_shape=(jax.ShapeDtypeStruct(distribution.shape, f32), jax.ShapeDtypeStruct((5, rows, cols), f32)),
            in_specs=[anywhere, vmem],
            out_specs=(anywhere, vmem),
            scratch_shapes=[
                pltpu.VMEM((count, rows + PAD, cols), f32),
                x_edge, x_edge, x_edge, x_edge,
                y_edge, y_edge, y_edge, y_edge,
                pltpu.VMEM((5, rows, cols), f32),
                pltpu.VMEM((owners, 5, SLAB, cols), f32),
                pltpu.VMEM((2, n_vert, 5, SLAB, cols), f32),
                pltpu.VMEM((2, 5, SLAB, cols), f32),
                pltpu.VMEM((2, owners, 5, SLAB, cols), f32),
                pltpu.VMEM((5, rows, cols), f32),
                pltpu.VMEM((VG, rows, cols), f32),
                pltpu.VMEM((6, PAD, cols), f32),
                pltpu.VMEM((6, PAD, cols), f32),
                pltpu.VMEM((VG // size, packed_rows, cols), f32),
            ]
            + [dma((chunks,))] * 10
            + [dma((2, owners)), dma((2, n_vert)), dma((2, n_vert)), dma((2, owners)), dma, dma],
            compiler_params=pltpu.CompilerParams(
                collective_id=0, has_side_effects=True, vmem_limit_bytes=56 * 1024 * 1024),
            name="stream",
        )(distribution, collision_rate)
    block = pl.BlockSpec((chunk_groups * size, rows, cols), lambda c: (c, 0, 0))
    return pl.pallas_call(
        functools.partial(relax, size, chunk_groups),
        out_shape=jax.ShapeDtypeStruct(distribution.shape, f32),
        grid=(chunks,),
        in_specs=[block, vmem, vmem],
        out_specs=block,
        scratch_shapes=[pltpu.VMEM((VG, rows, cols), f32)],
        compiler_params=pltpu.CompilerParams(vmem_limit_bytes=60 * 1024 * 1024),
        name="relax",
    )(moved, collision_rate, par)


def solution(mesh):
    placed = (P("vert", "gx", "gy"), P("gx", "gy"))
    return jax.shard_map(
        functools.partial(body, mesh), mesh=mesh, in_specs=placed, out_specs=P("vert", "gx", "gy"), check_vma=False)
```

```python
import functools
import math

import jax
import jax.numpy as jnp
from jax import lax
from jax.experimental import pallas as pl
from jax.experimental.pallas import tpu as pltpu
from jax.sharding import PartitionSpec as P

VG = 20
NZ = 2
SPEED_MAX = 4.5
DT = 0.3 / 4.5
STEP = 2.0 * SPEED_MAX / VG
WEIGHT = STEP**3 / (2.0 * math.pi) ** 1.5
MESH = pl.DeviceIdType.MESH
HALF = VG // 2
SLAB = 4
PAD = 8
SUB = 8
CHUNK = VG * VG // 2
BLOCK = 4


def speed_of(index):
    if isinstance(index, int):
        return STEP * (index + 0.5) - SPEED_MAX
    return STEP * (index.astype(jnp.float32) + 0.5) - SPEED_MAX


def group_place(first, group, size):
    start = first + group * size
    last = 0 if size == VG else lax.rem(start, VG)
    return start // (VG * VG), lax.rem(start // VG, VG), last


def amplitudes(ramp, flow_x, flow_y, inv, cx, cy):
    dx = cx - flow_x
    dy = cy - flow_y
    return ramp * jnp.exp(-inv * (dx * dx + dy * dy))


def stream(n_vert, size, chunk_groups, dist, rate, out, par_out, state, xs1, xh1, xs2, xh2, ys1, yh1, ys2, yh2,
           acc, mom, rs, pslab, ag, par, ez, hps, hpr, ezh, load_sem, out_sem,
           xs1_s, xs1_r, xs2_s, xs2_r, ys1_s, ys1_r, ys2_s, ys2_r, rs_s, rs_r, ag_s, ag_r, hp_s, hp_r):
    count, rows, cols = dist.shape
    groups = count // size
    chunks = groups // chunk_groups
    chunk_vel = chunk_groups * size
    owners = rows // SLAB
    gx, gy, me = lax.axis_index("gx"), lax.axis_index("gy"), lax.axis_index("vert")
    to_x = {"gx": 1 - gx}
    to_y = {"gy": 1 - gy}
    first = me * count
    x_up = me * 2 >= n_vert
    lane = lax.broadcasted_iota(jnp.int32, (rows, cols), 1)
    even = lane % NZ == 0
    slot = lane // (2 * NZ)

    def load(c):
        part = pl.ds(c * chunk_vel, chunk_vel)
        return pltpu.make_async_copy(dist.at[part], state.at[part, pl.ds(0, rows)], load_sem.at[c])

    def store(c):
        part = pl.ds(c * chunk_vel, chunk_vel)
        return pltpu.make_async_copy(state.at[part, pl.ds(0, rows)], out.at[part], out_sem.at[c])

    def send(src, dst, s_sem, r_sem, c, device):
        part = pl.ds(c * chunk_groups, chunk_groups)
        return pltpu.make_async_remote_copy(
            src_ref=src.at[part], dst_ref=dst.at[part], send_sem=s_sem.at[c], recv_sem=r_sem.at[c],
            device_id=device, device_id_type=MESH)

    def each(n, fn, low=0):
        lax.fori_loop(low, n, lambda c, z: (fn(c), z)[1], 0)

    each(chunks, lambda c: load(c).start())

    barrier = pltpu.get_barrier_semaphore()
    pl.semaphore_signal(barrier, inc=1, device_id=to_x, device_id_type=MESH)
    pl.semaphore_signal(barrier, inc=1, device_id=to_y, device_id_type=MESH)
    each(n_vert, lambda k: pl.semaphore_signal(
        barrier, inc=1, device_id={"vert": lax.rem(me + k, n_vert)}, device_id_type=MESH), 1)
    pl.semaphore_wait(barrier, n_vert + 1)

    def pack_chunk(c):
        load(c).wait()

        def pack(n, z):
            g = c * chunk_groups + n
            _, j, _ = group_place(first, g, size)
            turn = jnp.where(j >= HALF, 2 * NZ, 0)
            packed = jnp.zeros((rows, cols), jnp.float32)
            for t in range(size):
                v = g * size + t
                f = state[v, 0:rows, :]
                packed = jnp.where(slot == t, pltpu.roll(f, 2 * NZ * t + turn, 1), packed)
                xs1[g, 2 * t : 2 * t + 2, :] = jnp.where(x_up, f[rows - 2 : rows], f[0:2])
            ys1[g] = packed
            return z

        lax.fori_loop(0, chunk_groups, pack, 0)
        send(xs1, xh1, xs1_s, xs1_r, c, to_x).start()
        send(ys1, yh1, ys1_s, ys1_r, c, to_y).start()

    each(chunks, pack_chunk)

    def move_group(g, up, xh, yh, xs):
        i, j, l0 = group_place(first, g, size)
        cx, cy = speed_of(i), speed_of(j)
        ax, ay = DT * jnp.abs(cx), DT * jnp.abs(cy)
        y_up = j >= HALF
        turn = jnp.where(y_up, 2 * NZ, 0)
        near = jnp.where(y_up, NZ, cols - NZ)
        far = jnp.where(y_up, 2 * NZ, cols - 2 * NZ)
        edge = lax.rem(lane + turn, cols)
        edge_near = jnp.where(y_up, edge - NZ, edge)
        in_far = edge < 2 * NZ
        in_near = (edge_near >= 0) & (edge_near < NZ)
        base = 1.0 - 1.5 * ax - 1.5 * ay
        halo = yh[g]
        a = b = d = jnp.zeros((rows, cols), jnp.float32)
        tall = rows + PAD
        at = tall - 2 if up else rows
        for t in range(size):
            v = g * size + t
            state[v, at : at + 2, :] = xh[g, 2 * t : 2 * t + 2, :]
        for t in range(size):
            v = g * size + t
            az = 2.0 * DT * (abs(speed_of(t)) if size == VG else jnp.abs(speed_of(l0 + t)))
            whole = state[v]
            f = whole[0:rows]
            near_x = pltpu.roll(whole, 1 if up else tall - 1, 0)[0:rows]
            far_x = pltpu.roll(whole, 2 if up else tall - 2, 0)[0:rows]
            other = jnp.where(even, pltpu.roll(f, cols - 1, 1), pltpu.roll(f, 1, 1))
            edge_f = pltpu.roll(halo, lax.rem(2 * cols - 2 * NZ * t - turn, cols), 1)
            near_y = pltpu.roll(jnp.where(in_near, edge_f, f), near, 1)
            far_y = pltpu.roll(jnp.where(in_far, edge_f, f), far, 1)
            m = (base - az) * f + (2.0 * ax) * near_x - (0.5 * ax) * far_x
            m = m + ((2.0 * ay) * near_y - (0.5 * ay) * far_y + az * other)
            state[v, 0:rows, :] = m
            if xs is not None:
                xs[g, 2 * t : 2 * t + 2, :] = m[rows - 2 : rows] if up else m[0:2]
            a = a + m
            b = b + a
            d = d + b
        e = speed_of(l0) + STEP * size
        acc[0] += a
        acc[1] += cx * a
        acc[2] += cy * a
        acc[3] += e * a - STEP * b
        acc[4] += (cx * cx + cy * cy + e * e) * a - (2.0 * STEP * e + STEP * STEP) * b + (2.0 * STEP * STEP) * d

    def reduce_moments(step):
        for o in range(owners):
            for p in range(5):
                mom[o, p] = acc[p, SLAB * o : SLAB * (o + 1), :]

        def to_owner(o):
            return pltpu.make_async_remote_copy(
                src_ref=mom.at[o], dst_ref=rs.at[step, me], send_sem=rs_s.at[step, o], recv_sem=rs_r.at[step, me],
                device_id={"vert": o}, device_id_type=MESH)

        def from_device(s):
            return pltpu.make_async_remote_copy(
                src_ref=mom.at[0], dst_ref=rs.at[step, s], send_sem=rs_s.at[step, 0], recv_sem=rs_r.at[step, s],
                device_id={"vert": s}, device_id_type=MESH)

        def spread(s):
            return pltpu.make_async_remote_copy(
                src_ref=pslab.at[step], dst_ref=ag.at[step, me], send_sem=ag_s.at[step, s],
                recv_sem=ag_r.at[step, me], device_id={"vert": s}, device_id_type=MESH)

        def from_owner(o):
            return pltpu.make_async_remote_copy(
                src_ref=pslab.at[step], dst_ref=ag.at[step, o], send_sem=ag_s.at[step, 0],
                recv_sem=ag_r.at[step, o], device_id={"vert": o}, device_id_type=MESH)

        def others_owning(fn):
            def one(k):
                o = lax.rem(me + k, n_vert)
                if n_vert <= owners:
                    fn(o)
                else:
                    pl.when(o < owners)(lambda: fn(o))
            each(n_vert, one, 1)

        def others(fn):
            each(n_vert, lambda k: fn(lax.rem(me + k, n_vert)), 1)

        others_owning(lambda o: to_owner(o).start())

        def own():
            others(lambda s: from_device(s).wait_recv())

            def add(k, total):
                return total + rs[step, lax.rem(me + k, n_vert)]

            total = lax.fori_loop(1, n_vert, add, mom[me])
            mass = total[0]
            ux, uy, uz = total[1] / mass, total[2] / mass, total[3] / mass
            temper = (total[4] / mass - (ux * ux + uy * uy + uz * uz)) / 3.0
            pslab[step, 0] = WEIGHT * mass / (temper * jnp.sqrt(temper))
            pslab[step, 1] = ux
            pslab[step, 2] = uy
            pslab[step, 3] = uz
            pslab[step, 4] = 0.5 / temper
            others(lambda s: spread(s).start())
            ag[step, me] = pslab[step]

        if n_vert <= owners:
            own()
        else:
            pl.when(me < owners)(own)
        others_owning(lambda o: from_owner(o).wait_recv())
        for o in range(owners):
            for p in range(5):
                par[p, SLAB * o : SLAB * (o + 1), :] = ag[step, o, p]
        others_owning(lambda o: to_owner(o).wait_send())
        if n_vert <= owners:
            others(lambda s: spread(s).wait_send())
        else:
            pl.when(me < owners)(lambda: others(lambda s: spread(s).wait_send()))

    def move_first(c):
        send(ys1, yh1, ys1_s, ys1_r, c, to_y).wait_recv()
        send(xs1, xh1, xs1_s, xs1_r, c, to_x).wait_recv()
        for up in (True, False):
            @pl.when(x_up if up else jnp.logical_not(x_up))
            def _():
                each(chunk_groups, lambda n: move_group(c * chunk_groups + n, up, xh1, yh1, xs2))
        send(xs2, xh2, xs2_s, xs2_r, c, to_x).start()

    acc[...] = jnp.zeros_like(acc)
    each(chunks, move_first)
    reduce_moments(0)

    keep = 1.0 - rate[...]
    ramp = rate[...] * par[0]
    for p, value in enumerate((keep, ramp, par[1], par[2], par[3], par[4])):
        two = jnp.where(x_up, value[rows - 2 : rows], value[0:2])
        for q in range(PAD // 2):
            hps[p, 2 * q : 2 * q + 2, :] = two
    edges = pltpu.make_async_remote_copy(
        src_ref=hps, dst_ref=hpr, send_sem=hp_s, recv_sem=hp_r, device_id=to_x, device_id_type=MESH)
    edges.start()

    def fill_ez(l):
        dz = speed_of(l) - par[3]
        ez[l] = jnp.exp(-par[4] * dz * dz)

    each(VG, fill_ez)

    def collide_chunk(c):
        def collide(n, z):
            g = c * chunk_groups + n
            i, j, l0 = group_place(first, g, size)
            turn = jnp.where(j >= HALF, 2 * NZ, 0)
            keep = 1.0 - rate[...]
            amp = amplitudes(rate[...] * par[0], par[1], par[2], par[4], speed_of(i), speed_of(j))
            packed = jnp.zeros((rows, cols), jnp.float32)
            for t in range(size):
                v = g * size + t
                f = keep * state[v, 0:rows, :] + amp * ez[l0 + t]
                state[v, 0:rows, :] = f
                packed = jnp.where(slot == t, pltpu.roll(f, 2 * NZ * t + turn, 1), packed)
            ys2[g] = packed
            return z

        lax.fori_loop(0, chunk_groups, collide, 0)
        send(ys2, yh2, ys2_s, ys2_r, c, to_y).start()

    collide_chunk(0)

    edges.wait_recv()
    packed_rows = xh2.shape[1]
    for s in range(VG // size):
        for q in range(packed_rows // PAD):
            index = s * size + (lax.broadcasted_iota(jnp.int32, (PAD, cols), 0) + PAD * q) // 2
            dz = speed_of(index) - hpr[4]
            ezh[s, PAD * q : PAD * (q + 1), :] = jnp.exp(-hpr[5] * dz * dz)

    def collide_edge(g):
        i, j, l0 = group_place(first, g, size)
        amp = amplitudes(hpr[1], hpr[2], hpr[3], hpr[5], speed_of(i), speed_of(j))
        for q in range(packed_rows // PAD):
            part = slice(PAD * q, PAD * (q + 1))
            xh2[g, part, :] = hpr[0] * xh2[g, part, :] + amp * ezh[l0 // size, part, :]

    def move_second(c):
        send(ys2, yh2, ys2_s, ys2_r, c, to_y).wait_recv()
        send(xs2, xh2, xs2_s, xs2_r, c, to_x).wait_recv()
        each(chunk_groups, lambda n: collide_edge(c * chunk_groups + n))
        for up in (True, False):
            @pl.when(x_up if up else jnp.logical_not(x_up))
            def _():
                each(chunk_groups, lambda n: move_group(c * chunk_groups + n, up, xh2, yh2, None))
        store(c).start()

    acc[...] = jnp.zeros_like(acc)
    each(chunks, move_second)
    reduce_moments(1)
    par_out[...] = par[...]

    def finish(c):
        store(c).wait()
        send(xs1, xh1, xs1_s, xs1_r, c, to_x).wait_send()
        send(xs2, xh2, xs2_s, xs2_r, c, to_x).wait_send()
        send(ys1, yh1, ys1_s, ys1_r, c, to_y).wait_send()
        send(ys2, yh2, ys2_s, ys2_r, c, to_y).wait_send()

    each(chunks, finish)
    edges.wait_send()


def stream_rows(n_vert, dist, rate, out, par_out, T, U, ys1, yh1, ys2, yh2, tab, acc, mom, rs, pslab, ag, par, ez, ey,
                amp, hps, hpr, weights, load_sem, out_sem, xs1_s, xs1_r, xs2_s, xs2_r, ys1_s, ys1_r, ys2_s, ys2_r,
                rs_s, rs_r, ag_s, ag_r, hp_s, hp_r):
    count, rows, cols = dist.shape
    chunks = count // CHUNK
    per_chunk = CHUNK // SUB
    gx, gy, me = lax.axis_index("gx"), lax.axis_index("gy"), lax.axis_index("vert")
    to_x = {"gx": 1 - gx}
    to_y = {"gy": 1 - gy}
    first = me * count
    x_up = me * 2 >= n_vert
    sign = jnp.where(x_up, 1, -1)
    start = jnp.where(x_up, 2, rows + 1)
    edge_from = jnp.where(x_up, rows, 2)
    edge_to = jnp.where(x_up, 0, rows + 2)
    lane = lax.broadcasted_iota(jnp.int32, (SUB, cols), 1)
    sub = lax.broadcasted_iota(jnp.int32, (SUB, cols), 0)
    slot = lane // (2 * NZ)

    def row(k):
        return start + sign * k

    def each(n, fn, low=0):
        lax.fori_loop(low, n, lambda c, z: (fn(c), z)[1], 0)

    def span(c):
        return pl.ds(c * CHUNK, CHUNK)

    def load_start(c):
        each(rows, lambda x: pltpu.make_async_copy(
            dist.at[span(c), x, :], T.at[x + 2, span(c), :], load_sem.at[c]).start())

    def load_wait(c):
        inner = (pl.ds(2, rows), span(c))
        pltpu.make_async_copy(U.at[inner], T.at[inner], load_sem.at[c]).wait()

    def store_start(c):
        each(rows, lambda x: pltpu.make_async_copy(
            U.at[x + 2, span(c), :], out.at[span(c), x, :], out_sem.at[c]).start())

    def store_wait(c):
        inner = (pl.ds(2, rows), span(c))
        pltpu.make_async_copy(U.at[inner], T.at[inner], out_sem.at[c]).wait()

    def send_x(buf, s_sem, r_sem, c):
        return pltpu.make_async_remote_copy(
            src_ref=buf.at[pl.ds(edge_from, 2), span(c)], dst_ref=buf.at[pl.ds(edge_to, 2), span(c)],
            send_sem=s_sem.at[c], recv_sem=r_sem.at[c], device_id=to_x, device_id_type=MESH)

    def send_first(n):
        c, side = n // 2, lax.rem(n, 2)
        return pltpu.make_async_remote_copy(
            src_ref=dist.at[span(c), edge_from - 2 + side, :], dst_ref=T.at[edge_to + side, span(c), :],
            send_sem=xs1_s.at[n], recv_sem=xs1_r.at[n], device_id=to_x, device_id_type=MESH)

    def send_y(src, dst, s_sem, r_sem, c):
        part = pl.ds(c * per_chunk, per_chunk)
        return pltpu.make_async_remote_copy(
            src_ref=src.at[part], dst_ref=dst.at[part], send_sem=s_sem.at[c], recv_sem=r_sem.at[c],
            device_id=to_y, device_id_type=MESH)

    def chunk_place(c):
        begin = first + c * CHUNK
        return begin // (VG * VG), lax.rem(begin // CHUNK, 2)

    def by_half(half, fn):
        for up in (True, False):
            pl.when(half == (1 if up else 0))(functools.partial(fn, up))

    each(chunks, load_start)

    barrier = pltpu.get_barrier_semaphore()
    pl.semaphore_signal(barrier, inc=1, device_id=to_x, device_id_type=MESH)
    pl.semaphore_signal(barrier, inc=1, device_id=to_y, device_id_type=MESH)
    each(n_vert, lambda k: pl.semaphore_signal(
        barrier, inc=1, device_id={"vert": lax.rem(me + k, n_vert)}, device_id_type=MESH), 1)

    def fill_table(g):
        spot = (g * SUB + sub).astype(jnp.float32)
        j = jnp.floor((spot + 0.5) * (1.0 / VG))
        cy = STEP * (j + 0.5) - SPEED_MAX
        cz = STEP * (spot - VG * j + 0.5) - SPEED_MAX
        ay, az = DT * jnp.abs(cy), DT * jnp.abs(cz)
        tab[g, 0] = 1.0 - 1.5 * ay - 2.0 * az
        tab[g, 1] = 2.0 * ay
        tab[g, 2] = 2.0 * az
        tab[g, 3] = cy
        tab[g, 4] = cz
        tab[g, 5] = cy * cy + cz * cz

    each(2 * per_chunk, fill_table)

    def fill_weights():
        source = lax.broadcasted_iota(jnp.int32, (cols, cols), 0)
        target = lax.broadcasted_iota(jnp.int32, (cols, cols), 1)
        swap = jnp.where(source == target + 1 - 2 * (target % NZ), 1.0, 0.0).astype(jnp.bfloat16)
        for half, step in ((0, NZ), (1, -NZ)):
            along = jnp.where(source == target + step, 1.0, jnp.where(source == target + 2 * step, -0.25, 0.0))
            for part in range(2):
                at = slice(part * cols, (part + 1) * cols)
                weights[half, at, 0:cols] = along.astype(jnp.bfloat16)
                weights[half, at, cols : 2 * cols] = swap

    fill_weights()
    pl.semaphore_wait(barrier, n_vert + 1)
    each(2 * chunks, lambda n: send_first(n).start())

    def pack_chunk(c):
        load_wait(c)
        _, half = chunk_place(c)

        def run(up):
            def pack(n):
                at = pl.ds(pl.multiple_of(c * CHUNK + n * SUB, SUB), SUB)
                packed = jnp.zeros((SUB, cols), jnp.float32)
                for k in range(rows):
                    turned = pltpu.roll(T[row(k), at, :], (2 * NZ * k + (2 * NZ if up else 0)) % cols, 1)
                    packed = jnp.where(slot == k, turned, packed)
                ys1[c * per_chunk + n] = packed

            each(per_chunk, pack)

        by_half(half, run)
        send_y(ys1, yh1, ys1_s, ys1_r, c).start()

    def move_chunk(c, yh):
        i, half = chunk_place(c)
        cx = speed_of(i)
        ax = DT * jnp.abs(cx)

        def run(up):
            outer = 0 if up else cols - 2 * NZ
            in_edge = lane < 2 * NZ if up else lane >= outer
            inside = lane % (2 * NZ)

            def from_edges(g):
                halo = yh[g]
                if up:
                    return jnp.where(inside < NZ, pltpu.roll(halo, cols - NZ, 1), 0.0) - 0.25 * halo
                return jnp.where(inside >= NZ, pltpu.roll(halo, NZ, 1), 0.0) - 0.25 * halo

            def block(kb):
                k0 = kb * BLOCK

                f = [T[row(k0 + kk), span(c), :] for kk in range(-2, BLOCK)]
                mid = jnp.concatenate(f[2:], axis=0)
                high = mid.astype(jnp.bfloat16)
                low = (mid - high.astype(jnp.float32)).astype(jnp.bfloat16)
                mixed = jnp.dot(jnp.concatenate([high, low], axis=1), weights[1 if up else 0],
                                preferred_element_type=jnp.float32)
                sums = [jnp.zeros((SUB, cols), jnp.float32)] * (4 * BLOCK)
                for n in range(per_chunk):
                    at = pl.ds(pl.multiple_of(c * CHUNK + n * SUB, SUB), SUB)
                    place = half * per_chunk + n
                    c0 = tab[place, 0] - 1.5 * ax
                    by, bz = tab[place, 1], tab[place, 2]
                    cy, cz, cq = tab[place, 3], tab[place, 4], tab[place, 5]
                    terms = from_edges(c * per_chunk + n)
                    own = slice(n * SUB, (n + 1) * SUB)
                    for kk in range(BLOCK):
                        far_x, near_x, here = f[kk][own], f[kk + 1][own], f[kk + 2][own]
                        back = lax.rem(outer + cols - 2 * NZ * (k0 + kk), cols)
                        edge = jnp.where(in_edge, pltpu.roll(terms, back, 1), 0.0)
                        got = slice(kk * CHUNK + n * SUB, kk * CHUNK + (n + 1) * SUB)
                        m = (c0 * here + (2.0 * ax) * (near_x - 0.25 * far_x)) + (
                            by * (mixed[got, 0:cols] + edge) + bz * mixed[got, cols : 2 * cols])
                        U[row(k0 + kk), at, :] = m
                        sums[4 * kk] = sums[4 * kk] + m
                        sums[4 * kk + 1] = sums[4 * kk + 1] + cy * m
                        sums[4 * kk + 2] = sums[4 * kk + 2] + cz * m
                        sums[4 * kk + 3] = sums[4 * kk + 3] + cq * m
                for kk in range(BLOCK):
                    x = row(k0 + kk) - 2
                    a, my, mz, mq = sums[4 * kk : 4 * kk + 4]
                    acc[0, x] += a
                    acc[1, x] += cx * a
                    acc[2, x] += my
                    acc[3, x] += mz
                    acc[4, x] += (cx * cx) * a + mq

            each(rows // BLOCK, block)

        by_half(half, run)

    def reduce_moments(step):
        for o in range(n_vert):
            for p in range(5):
                mom[o, p] = jnp.sum(acc[p, SLAB * o : SLAB * (o + 1)], axis=1)

        def to_owner(o):
            return pltpu.make_async_remote_copy(
                src_ref=mom.at[o], dst_ref=rs.at[step, me], send_sem=rs_s.at[step, o], recv_sem=rs_r.at[step, me],
                device_id={"vert": o}, device_id_type=MESH)

        def from_device(s):
            return pltpu.make_async_remote_copy(
                src_ref=mom.at[s], dst_ref=rs.at[step, s], send_sem=rs_s.at[step, s], recv_sem=rs_r.at[step, s],
                device_id={"vert": s}, device_id_type=MESH)

        def spread(s):
            return pltpu.make_async_remote_copy(
                src_ref=pslab.at[step], dst_ref=ag.at[step, me], send_sem=ag_s.at[step, s],
                recv_sem=ag_r.at[step, me], device_id={"vert": s}, device_id_type=MESH)

        def from_owner(o):
            return pltpu.make_async_remote_copy(
                src_ref=pslab.at[step], dst_ref=ag.at[step, o], send_sem=ag_s.at[step, o],
                recv_sem=ag_r.at[step, o], device_id={"vert": o}, device_id_type=MESH)

        def others(fn):
            each(n_vert, lambda k: fn(lax.rem(me + k, n_vert)), 1)

        others(lambda o: to_owner(o).start())
        others(lambda s: from_device(s).wait_recv())
        total = lax.fori_loop(1, n_vert, lambda k, t: t + rs[step, lax.rem(me + k, n_vert)], mom[me])
        mass = total[0]
        ux, uy, uz = total[1] / mass, total[2] / mass, total[3] / mass
        temper = (total[4] / mass - (ux * ux + uy * uy + uz * uz)) / 3.0
        pslab[step, 0] = WEIGHT * mass / (temper * jnp.sqrt(temper))
        pslab[step, 1] = ux
        pslab[step, 2] = uy
        pslab[step, 3] = uz
        pslab[step, 4] = 0.5 / temper
        others(lambda s: spread(s).start())
        ag[step, me] = pslab[step]
        others(lambda o: from_owner(o).wait_recv())
        others(lambda o: to_owner(o).wait_send())
        others(lambda s: spread(s).wait_send())

    def move_first(c):
        pl.when(c + 1 < chunks)(lambda: pack_chunk(c + 1))
        send_y(ys1, yh1, ys1_s, ys1_r, c).wait_recv()
        send_first(2 * c).wait_recv()
        send_first(2 * c + 1).wait_recv()
        move_chunk(c, yh1)
        send_x(U, xs2_s, xs2_r, c).start()

    acc[...] = jnp.zeros_like(acc)
    pack_chunk(0)
    each(chunks, move_first)
    reduce_moments(0)

    par[...] = jnp.ones_like(par)
    par[0, 2 : rows + 2, :] = 1.0 - rate[...]
    for o in range(n_vert):
        at = slice(SLAB * o + 2, SLAB * (o + 1) + 2)
        par[1, at, :] = rate[SLAB * o : SLAB * (o + 1), :] * ag[0, o, 0]
        for p in range(1, 5):
            par[p + 1, at, :] = ag[0, o, p]
    for p in range(6):
        hps[p] = jnp.where(x_up, par[p, rows : rows + 2, :], par[p, 2:4, :])
    edges = pltpu.make_async_remote_copy(
        src_ref=hps, dst_ref=hpr, send_sem=hp_s, recv_sem=hp_r, device_id=to_x, device_id_type=MESH)
    edges.start()

    def fill_ey():
        def one(j):
            dy = speed_of(j) - par[3]
            ey[j] = jnp.exp(-par[5] * dy * dy)
        each(VG, one)

    def fill_ez(r):
        for q in range(5):
            dz = tab[q, 4] - par[4, pl.ds(r, 1), :]
            ez[q, r] = jnp.exp(-par[5, pl.ds(r, 1), :] * dz * dz)

    def fill_amp(c):
        i, half = chunk_place(c)
        dx = speed_of(i) - par[2]
        front = par[1] * jnp.exp(-par[5] * dx * dx)
        for j in range(VG // 2):
            amp[j] = front * ey[half * (VG // 2) + j]

    def collided(c, sb, r):
        low = jnp.broadcast_to(amp[2 * sb, pl.ds(r, 1), :], (SUB, cols))
        high = jnp.broadcast_to(amp[2 * sb + 1, pl.ds(r, 1), :], (SUB, cols))
        keep = jnp.broadcast_to(par[0, pl.ds(r, 1), :], (SUB, cols))
        mixed = jnp.where(sub < SUB // 2, low, high)
        found = []
        for q, front in enumerate((low, low, mixed, high, high)):
            at = pl.ds(pl.multiple_of(c * CHUNK + (sb * 5 + q) * SUB, SUB), SUB)
            f = keep * U[r, at, :] + front * ez[q, r]
            T[r, at, :] = f
            found.append(f)
        return found

    fill_ey()
    each(rows, lambda x: fill_ez(x + 2))

    def collide_chunk(c):
        _, half = chunk_place(c)
        fill_amp(c)

        def run(up):
            def five(sb):
                def some(packed):
                    packed = list(packed)
                    for k in range(rows):
                        turn = (2 * NZ * k + (2 * NZ if up else 0)) % cols
                        here = slot == k
                        for q, f in enumerate(collided(c, sb, row(k))):
                            packed[q] = jnp.where(here, pltpu.roll(f, turn, 1), packed[q])
                    return tuple(packed)

                zero = jnp.zeros((SUB, cols), jnp.float32)
                packed = some((zero,) * 5)
                for q in range(5):
                    ys2[c * per_chunk + sb * 5 + q] = packed[q]

            each(per_chunk // 5, five)

        by_half(half, run)
        send_y(ys2, yh2, ys2_s, ys2_r, c).start()

    collide_chunk(0)

    edges.wait_recv()
    for p in range(6):
        par[p, 0:2, :] = hpr[p]
        par[p, rows + 2 : rows + 4, :] = hpr[p]
    fill_ey()
    each(2, lambda x: fill_ez(edge_to + x))

    def move_second(c):
        pl.when(c + 1 < chunks)(lambda: collide_chunk(c + 1))
        send_y(ys2, yh2, ys2_s, ys2_r, c).wait_recv()
        send_x(U, xs2_s, xs2_r, c).wait_recv()
        send_x(U, xs2_s, xs2_r, c).wait_send()
        fill_amp(c)

        def edge(sb):
            collided(c, sb, edge_to)
            collided(c, sb, edge_to + 1)

        each(per_chunk // 5, edge)
        move_chunk(c, yh2)
        store_start(c)

    acc[...] = jnp.zeros_like(acc)
    each(chunks, move_second)
    reduce_moments(1)
    for o in range(n_vert):
        for p in range(5):
            par_out[p, SLAB * o : SLAB * (o + 1), :] = ag[1, o, p]

    def finish(c):
        store_wait(c)
        send_y(ys1, yh1, ys1_s, ys1_r, c).wait_send()
        send_y(ys2, yh2, ys2_s, ys2_r, c).wait_send()

    each(chunks, finish)
    each(2 * chunks, lambda n: send_first(n).wait_send())
    edges.wait_send()


def run_rows(n_vert, distribution, collision_rate):
    count, rows, cols = distribution.shape
    chunks, groups = count // CHUNK, count // SUB
    f32 = jnp.float32
    state = pltpu.VMEM((rows + 4, count, cols), f32)
    y_edge = pltpu.VMEM((groups, SUB, cols), f32)
    dma = pltpu.SemaphoreType.DMA
    vmem = pl.BlockSpec(memory_space=pltpu.VMEM)
    anywhere = pl.BlockSpec(memory_space=pl.ANY)
    return pl.pallas_call(
        functools.partial(stream_rows, n_vert),
        out_shape=(jax.ShapeDtypeStruct(distribution.shape, f32), jax.ShapeDtypeStruct((5, rows, cols), f32)),
        in_specs=[anywhere, vmem],
        out_specs=(anywhere, vmem),
        scratch_shapes=[
            state, state, y_edge, y_edge, y_edge, y_edge,
            pltpu.VMEM((2 * CHUNK // SUB, 6, SUB, cols), f32),
            pltpu.VMEM((5, rows, SUB, cols), f32),
            pltpu.VMEM((n_vert, 5, SLAB, cols), f32),
            pltpu.VMEM((2, n_vert, 5, SLAB, cols), f32),
            pltpu.VMEM((2, 5, SLAB, cols), f32),
            pltpu.VMEM((2, n_vert, 5, SLAB, cols), f32),
            pltpu.VMEM((6, rows + 4, cols), f32),
            pltpu.VMEM((5, rows + 4, SUB, cols), f32),
            pltpu.VMEM((VG, rows + 4, cols), f32),
            pltpu.VMEM((VG // 2, rows + 4, cols), f32),
            pltpu.VMEM((6, 2, cols), f32),
            pltpu.VMEM((6, 2, cols), f32),
            pltpu.VMEM((2, 2 * cols, 2 * cols), jnp.bfloat16),
        ]
        + [dma((chunks,))] * 2 + [dma((2 * chunks,))] * 2 + [dma((chunks,))] * 6
        + [dma((2, n_vert))] * 4 + [dma, dma],
        compiler_params=pltpu.CompilerParams(
            collective_id=1, has_side_effects=True, vmem_limit_bytes=56 * 1024 * 1024),
        name="stream_rows",
    )(distribution, collision_rate)


def relax(size, chunk_groups, moved, rate, par, out, ez):
    step = pl.program_id(0)
    first = lax.axis_index("vert") * (pl.num_programs(0) * chunk_groups * size)

    @pl.when(step == 0)
    def _():
        def fill(l, z):
            dz = speed_of(l) - par[3]
            ez[l] = jnp.exp(-par[4] * dz * dz)
            return z
        lax.fori_loop(0, VG, fill, 0)

    keep = 1.0 - rate[...]
    for n in range(chunk_groups):
        i, j, l0 = group_place(first, step * chunk_groups + n, size)
        amp = amplitudes(rate[...] * par[0], par[1], par[2], par[4], speed_of(i), speed_of(j))
        for t in range(size):
            out[n * size + t] = keep * moved[n * size + t] + amp * ez[l0 + t]


def body(mesh, distribution, collision_rate):
    count, rows, cols = distribution.shape
    n_vert = mesh.shape["vert"]
    size = math.gcd(count, VG)
    groups = count // size
    chunk_groups = math.gcd(groups, 5)
    chunks = groups // chunk_groups
    packed_rows = -(-2 * size // PAD) * PAD
    owners = rows // SLAB
    f32 = jnp.float32
    x_edge = pltpu.VMEM((groups, packed_rows, cols), f32)
    y_edge = pltpu.VMEM((groups, rows, cols), f32)
    dma = pltpu.SemaphoreType.DMA
    vmem = pl.BlockSpec(memory_space=pltpu.VMEM)
    anywhere = pl.BlockSpec(memory_space=pl.ANY)
    if count % CHUNK == 0 and rows == SLAB * n_vert:
        moved, par = run_rows(n_vert, distribution, collision_rate)
    else:
        moved, par = pl.pallas_call(
            functools.partial(stream, n_vert, size, chunk_groups),
            out_shape=(jax.ShapeDtypeStruct(distribution.shape, f32), jax.ShapeDtypeStruct((5, rows, cols), f32)),
            in_specs=[anywhere, vmem],
            out_specs=(anywhere, vmem),
            scratch_shapes=[
                pltpu.VMEM((count, rows + PAD, cols), f32),
                x_edge, x_edge, x_edge, x_edge,
                y_edge, y_edge, y_edge, y_edge,
                pltpu.VMEM((5, rows, cols), f32),
                pltpu.VMEM((owners, 5, SLAB, cols), f32),
                pltpu.VMEM((2, n_vert, 5, SLAB, cols), f32),
                pltpu.VMEM((2, 5, SLAB, cols), f32),
                pltpu.VMEM((2, owners, 5, SLAB, cols), f32),
                pltpu.VMEM((5, rows, cols), f32),
                pltpu.VMEM((VG, rows, cols), f32),
                pltpu.VMEM((6, PAD, cols), f32),
                pltpu.VMEM((6, PAD, cols), f32),
                pltpu.VMEM((VG // size, packed_rows, cols), f32),
            ]
            + [dma((chunks,))] * 10
            + [dma((2, owners)), dma((2, n_vert)), dma((2, n_vert)), dma((2, owners)), dma, dma],
            compiler_params=pltpu.CompilerParams(
                collective_id=0, has_side_effects=True, vmem_limit_bytes=56 * 1024 * 1024),
            name="stream",
        )(distribution, collision_rate)
    block = pl.BlockSpec((chunk_groups * size, rows, cols), lambda c: (c, 0, 0))
    return pl.pallas_call(
        functools.partial(relax, size, chunk_groups),
        out_shape=jax.ShapeDtypeStruct(distribution.shape, f32),
        grid=(chunks,),
        in_specs=[block, vmem, vmem],
        out_specs=block,
        scratch_shapes=[pltpu.VMEM((VG, rows, cols), f32)],
        compiler_params=pltpu.CompilerParams(vmem_limit_bytes=32 * 1024 * 1024),
        name="relax",
    )(moved, collision_rate, par)


def solution(mesh):
    placed = (P("vert", "gx", "gy"), P("gx", "gy"))
    return jax.shard_map(
        functools.partial(body, mesh), mesh=mesh, in_specs=placed, out_specs=P("vert", "gx", "gy"), check_vma=False)
```
